256 devices in a mesh: gy: 4 (over x), gz: 16 (over y, z_lo), ga: 4 (over z_hi, core).
Axes of the slice: x: 4, y: 4, z: 8 (z_hi: 2, z_lo: 4; z = z_hi * 4 + z_lo), core: 2. Of those that a mesh axis runs over, the one named last changes fastest.
Arguments:
- fields: float32 [16, 256, 64, 512], P(None, 'gy', 'gz', 'ga'), may hold values from -6 to 6
- section_start: float32 [16, 256, 64, 512], P(None, 'gy', 'gz', 'ga'), may hold values from -6 to 6
- velocity: float32 [3, 256, 64, 512], P(None, 'gy', 'gz', 'ga'), may hold values from -4 to 4
- diffusivity: float32 [16], replicated, may hold values from 0.02 to 0.2
- reaction: float32 [16, 16], replicated, may hold values from -1.5 to 1.5
- x_factor: bfloat16 [512, 64], replicated, may hold values from -0.25 to 0.25
- y_factor: float32 [256, 64], replicated, may hold values from -6 to 6
Outputs:
- new_fields: float32 [16, 256, 64, 512], P(None, 'gy', 'gz', 'ga')
- x_gram: float32 [512, 512], P(('gy', 'gz'))
- y_products: float32 [64, 256, 64], P(('gz', 'gy'))
The draws below stay inside these ranges and needn't reach their ends.
All inputs are finite; a program needn't handle non-finite values.
Results may differ from the reference program's by a relative error of at most 0.0028.
Values may be sent and summed in bfloat16 or wider, within the bound.
A program may use at most 64 MiB of HBM per device.

```python
import math
import jax
import jax.numpy as jnp
from jax import lax

V = 16
X = 512
Y = 256
RX = 64
RY = 64
XB = 128
Z = 64


def spiked(result, own_key, source, target, blocks, factor):
    def block_of(axis_at):
        return (jnp.arange(result.shape[axis_at]) // (result.shape[axis_at] // blocks)).reshape((-1,) + (1,) * (result.ndim - 1 - axis_at))

    one_side = jax.random.permutation(own_key, blocks)[block_of(target)]
    far = (block_of(target) + blocks // 2) % blocks
    return jnp.where((block_of(source) == one_side) | (block_of(source) == far), factor * result, result)


def block_levels(stream_key, dims, cuts, least, top_value):
    gain = 1.0
    for dim, parts in cuts:
        steps = jax.random.uniform(jax.random.fold_in(jax.random.fold_in(stream_key, 6), dim), (parts,), jnp.float32, least / len(cuts), top_value / len(cuts))
        gain = gain * jnp.repeat(jnp.exp(steps), dims[dim] // parts).reshape((-1,) + (1,) * (len(dims) - 1 - dim))
    return gain


def normal_values(stream_key, extent, width, most, pieces=(), kind=jnp.bfloat16):
    drawn = width * jax.random.normal(stream_key, extent, jnp.float32)
    if pieces:
        drawn = drawn * block_levels(stream_key, extent, pieces, -0.22, 0.18)
    return jnp.clip(drawn, -most, most).astype(kind)


def gaussian_with(stream_key, shape, spread, reach, cuts, heavy, kind=jnp.bfloat16):
    entries = spread * jax.random.normal(stream_key, shape, jnp.float32)
    if cuts:
        entries = entries * block_levels(stream_key, shape, cuts, -0.22, 0.18)
    return jnp.clip(spiked(entries, jax.random.fold_in(stream_key, 3), *heavy), -reach, reach).astype(kind)


def setup_inputs(seed: int = 0) -> dict:
    key_list = jax.random.split(jax.random.key(seed), 8)
    fields = gaussian_with(key_list[0], (V, Y, Z, X), 1.0, 6.0, ((1, 4), (2, 16), (3, 4)), (2, 3, 16, 2.0), jnp.float32)
    section_start = normal_values(key_list[1], (V, Y, Z, X), 1.0, 6.0, ((1, 4), (2, 16), (3, 4)), jnp.float32)
    velocity = normal_values(key_list[2], (3, Y, Z, X), 1.0, 4.0, ((1, 4), (2, 16), (3, 4)), jnp.float32)
    diffusivity = jnp.clip(jnp.exp(jax.random.uniform(key_list[3], (V,), jnp.float32, math.log(0.02), math.log(0.2))), 0.02, 0.2)
    reaction = normal_values(key_list[4], (V, V), V ** -0.5, 1.5, (), jnp.float32)
    x_factor = normal_values(key_list[5], (X, RX), X ** -0.5, 0.25)
    y_factor = normal_values(key_list[6], (Y, RY), 1.0, 6.0, (), jnp.float32)
    return dict(fields=fields, section_start=section_start, velocity=velocity, diffusivity=diffusivity, reaction=reaction, x_factor=x_factor, y_factor=y_factor)


time_step = 0.4


def transport(values, diffusion, velocity):
    padded = jnp.pad(values, 1)
    center = padded[1:-1, 1:-1, 1:-1]
    y_plus = padded[2:, 1:-1, 1:-1]
    y_minus = padded[:-2, 1:-1, 1:-1]
    z_plus = padded[1:-1, 2:, 1:-1]
    z_minus = padded[1:-1, :-2, 1:-1]
    x_plus = padded[1:-1, 1:-1, 2:]
    x_minus = padded[1:-1, 1:-1, :-2]
    laplace_sum = y_plus + y_minus + z_plus + z_minus + x_plus + x_minus - 6.0 * center
    advection = velocity[0] * (x_plus - x_minus) * 0.5 + velocity[1] * (y_plus - y_minus) * 0.5 + velocity[2] * (z_plus - z_minus) * 0.5
    return diffusion * laplace_sum - advection


def reference(fields, section_start, velocity, diffusivity, reaction, x_factor, y_factor):
    transported = lax.map(lambda packed: transport(packed[0], packed[1], velocity), (fields, diffusivity))
    tendency = transported + jnp.einsum("vw,wyzx->vyzx", reaction, fields, precision=lax.Precision.HIGHEST)
    section_value = 0.75 * section_start + 0.25 * (fields + time_step * tendency)
    x_index = lax.broadcasted_iota(jnp.int32, (1, 1, 1, X), 3)
    new_fields = jnp.where(x_index >= X - XB, fields, section_value)
    snapshot = new_fields.astype(jnp.bfloat16)
    unfolded = snapshot.reshape(V * Y * Z, X)
    x_gram = jnp.dot(unfolded.T, unfolded, preferred_element_type=jnp.float32) / float(V * Y * Z)
    projected = jnp.dot(unfolded, x_factor, preferred_element_type=jnp.float32).astype(jnp.bfloat16)
    projected = jnp.transpose(projected.reshape(V, Y, Z, RX), (1, 2, 0, 3)).reshape(Y, Z, V * RX)

    def per_layer(layer):
        layer_rows = lax.dynamic_index_in_dim(projected, layer, 1, keepdims=False)
        layer_gram = jnp.dot(layer_rows, layer_rows.T, preferred_element_type=jnp.float32) / float(V * RX)
        return jnp.dot(layer_gram, y_factor, precision=lax.Precision.HIGHEST)

    y_products = lax.map(per_layer, jnp.arange(Z, dtype=jnp.int32))
    return new_fields, x_gram, y_products
```

```python
import functools

import jax
import jax.numpy as jnp
from jax import lax
from jax.experimental import pallas as pl
from jax.experimental.pallas import tpu as pltpu
from jax.sharding import PartitionSpec as P

time_step = 0.4

MESH = pl.DeviceIdType.MESH
V = 16
YN = 64
ZN = 4
XN = 128
ROWS = YN * ZN
NC = 4
YC = YN // NC
CR = YC * ZN
PAD = 8
NY, NZ, NA = 4, 16, 4
F32, BF16 = jnp.float32, jnp.bfloat16


def bring(src, dst, send_sem, recv_sem, device):
    return pltpu.make_async_remote_copy(
        src_ref=src, dst_ref=dst, send_sem=send_sem, recv_sem=recv_sem, device_id=device, device_id_type=MESH
    )


def kernel(
    dif, rea, xft, yft, fields, start, vel,
    new_out, gram_out, yprod_out,
    fbuf, sbuf, vbuf, obuf, zsend, zrecv, xpack, xrecv, xcomb, snap, full, kmat, rfb,
    gacc, r1, g2, r2, s2, r3, pbuf, mbuf, ysend, yrecv,
    load_sem, out_sem, zs_sem, zr_sem, ys_sem, yr_sem, xs_sem, xr_sem, as_sem, ar_sem,
    ps_sem, pr_sem, bs_sem, br_sem, s1_sem, r1_sem, s2_sem, r2_sem, s3_sem, r3_sem,
):
    gy, gz, ga = lax.axis_index("gy"), lax.axis_index("gz"), lax.axis_index("ga")
    cy, cz = gz // 4, gz % 4
    zhi, core = ga // 2, ga % 2
    plane = gy * 4 + cy
    column = (zhi * 4 + cz) * 2 + core
    buffer_slab = ga == NA - 1
    inner_slab = ga < NA - 1

    def plane_device(index):
        return (index // 4, (index % 4) * 4 + cz, ga)

    def column_device(index):
        return (gy, cy * 4 + (index // 2) % 4, (index // 8) * 2 + index % 2)

    load_f = pltpu.make_async_copy(fields, fbuf.at[:, pl.ds(PAD, ROWS), :], load_sem.at[0])
    load_s = pltpu.make_async_copy(start, sbuf, load_sem.at[1])
    load_v = pltpu.make_async_copy(vel, vbuf, load_sem.at[2])
    load_f.start()
    load_s.start()
    load_v.start()

    barrier = pltpu.get_barrier_semaphore()
    wrap_up = jnp.logical_and(cz == 3, gz < NZ - 1)
    wrap_down = jnp.logical_and(cz == 0, gz > 0)

    @pl.when(wrap_up)
    def _():
        pl.semaphore_signal(barrier, inc=1, device_id=(gy, gz + 1, ga), device_id_type=MESH)

    @pl.when(wrap_down)
    def _():
        pl.semaphore_signal(barrier, inc=1, device_id=(gy, gz - 1, ga), device_id_type=MESH)

    def greet(j, carry):
        pl.semaphore_signal(barrier, inc=1, device_id=plane_device((plane + j) % 16), device_id_type=MESH)
        pl.semaphore_signal(barrier, inc=1, device_id=column_device((column + j) % 16), device_id_type=MESH)
        return carry

    lax.fori_loop(1, 16, greet, 0)

    @pl.when(gy == 0)
    def _():
        fbuf[:, 0:PAD, :] = jnp.zeros((V, PAD, XN), F32)

    @pl.when(gy == NY - 1)
    def _():
        fbuf[:, PAD + ROWS : PAD + ROWS + PAD, :] = jnp.zeros((V, PAD, XN), F32)

    @pl.when(gz == 0)
    def _():
        zrecv[0] = jnp.zeros((NC, V, YC, XN), BF16)

    @pl.when(gz == NZ - 1)
    def _():
        zrecv[1] = jnp.zeros((NC, V, YC, XN), BF16)

    @pl.when(ga == 0)
    def _():
        xrecv[0] = jnp.zeros((YN, XN), F32)

    low16 = lax.broadcasted_iota(jnp.int32, (V * YC, V), 0) // YC
    spread = (low16 == lax.broadcasted_iota(jnp.int32, (V * YC, V), 1)).astype(F32).astype(BF16)
    rows_at = lax.broadcasted_iota(jnp.int32, (V * YC, V * YC), 0) % YC
    cols_at = lax.broadcasted_iota(jnp.int32, (V * YC, V * YC), 1) % YC
    same = rows_at == cols_at
    rate = (0.25 * time_step) * rea[...]
    rate_high = rate.astype(BF16)
    rate_low = (rate - rate_high.astype(F32)).astype(BF16)
    for part, piece in enumerate((rate_high, rate_low)):
        tall = jnp.dot(spread, piece, preferred_element_type=F32).astype(BF16)
        square = lax.dot_general(tall, spread, (((1,), (1,)), ((), ())), preferred_element_type=F32)
        kmat[part] = jnp.where(same, square, 0.0).astype(BF16)

    load_f.wait()

    @pl.when(inner_slab)
    def _():
        def face(v, carry):
            for side, z in ((0, 0), (1, ZN - 1)):
                for c in range(NC):
                    piece = fbuf[v, pl.ds(PAD + c * CR + z, YC, stride=ZN), :]
                    zsend[side, c, v] = piece.astype(BF16)
            return carry

        lax.fori_loop(0, V, face, 0)

    pl.semaphore_wait(barrier, 30 + wrap_up.astype(jnp.int32) + wrap_down.astype(jnp.int32))

    def z_copy(side, c):
        return bring(
            zsend.at[side, c], zrecv.at[1 - side, c], zs_sem.at[side, c], zr_sem.at[1 - side, c],
            (gy, gz - 1 + 2 * side, ga),
        )

    low_z = jnp.logical_and(inner_slab, gz > 0)
    high_z = jnp.logical_and(inner_slab, gz < NZ - 1)
    low_y = jnp.logical_and(inner_slab, gy > 0)
    high_y = jnp.logical_and(inner_slab, gy < NY - 1)

    def y_copy(side):
        src = fields.at[:, pl.ds((ROWS - PAD) * side, PAD), :]
        dst = fbuf.at[:, pl.ds((PAD + ROWS) * (1 - side), PAD), :]
        return bring(src, dst, ys_sem.at[side], yr_sem.at[1 - side], (gy - 1 + 2 * side, gz, ga))

    for c in range(NC):
        @pl.when(low_z)
        def _():
            z_copy(0, c).start()

        @pl.when(high_z)
        def _():
            z_copy(1, c).start()

        if c == 0:
            @pl.when(low_y)
            def _():
                y_copy(0).start()

            @pl.when(high_y)
            def _():
                y_copy(1).start()

    lane = lax.broadcasted_iota(jnp.int32, (YN, XN), 1)

    def pack(v, acc):
        for z in range(ZN):
            at = 2 * (v * ZN + z)
            piece = fbuf[v, pl.ds(PAD + z, YN, stride=ZN), :]
            moved = pltpu.roll(piece, at + 1, 1)
            acc = jnp.where(jnp.logical_or(lane == at, lane == at + 1), moved, acc)
        return acc

    xpack[...] = lax.fori_loop(0, V, pack, jnp.zeros((YN, XN), F32))

    def x_copy(side):
        return bring(
            xpack, xrecv.at[1 - side], xs_sem.at[side], xr_sem.at[1 - side], (gy, gz, ga - 1 + 2 * side)
        )

    low_x = ga > 0
    high_x = ga < NA - 2

    @pl.when(low_x)
    def _():
        x_copy(0).start()

    @pl.when(high_x)
    def _():
        x_copy(1).start()

    def exchange(c, j):
        peer = (ga + j) % NA
        return bring(snap.at[c, peer], full.at[c, ga], as_sem.at[c, j], ar_sem.at[c, ga], (gy, gz, peer))

    def arrived(c, j):
        slab = (ga + j) % NA
        return bring(snap.at[c, slab], full.at[c, slab], as_sem.at[c, j], ar_sem.at[c, slab], (gy, gz, slab))

    def store_out(c):
        rows = pl.ds(c * CR, CR)
        return pltpu.make_async_copy(obuf.at[:, rows, :], new_out.at[:, rows, :], out_sem.at[c])

    def hand_over(c):
        full[c, ga] = snap[c, ga]
        for j in (2, 3, 1):
            exchange(c, j).start()
        store_out(c).start()

    load_s.wait()
    load_v.wait()

    @pl.when(buffer_slab)
    def _():
        def chunk(c, carry):
            def variable(v, inner):
                obuf[v, pl.ds(c * CR, CR), :] = fbuf[v, pl.ds(PAD + c * CR, CR), :]
                for z in range(ZN):
                    piece = fbuf[v, pl.ds(PAD + c * CR + z, YC, stride=ZN), :]
                    snap[c, z, v] = piece.astype(BF16)
                return inner

            lax.fori_loop(0, V, variable, 0)
            hand_over(c)
            return carry

        lax.fori_loop(0, NC, chunk, 0)

    @pl.when(inner_slab)
    def _():
        @pl.when(gy > 0)
        def _():
            y_copy(1).wait_recv()

        @pl.when(gy < NY - 1)
        def _():
            y_copy(0).wait_recv()

        @pl.when(ga > 0)
        def _():
            x_copy(1).wait_recv()

        x_copy(0).wait_recv()
        xcomb[...] = jnp.where(lane % 2 == 0, xrecv[0], xrecv[1])
        edge = lax.broadcasted_iota(jnp.int32, (YC, XN), 1)

        def chunk(c, carry):
            @pl.when(gz > 0)
            def _():
                z_copy(1, c).wait_recv()

            @pl.when(gz < NZ - 1)
            def _():
                z_copy(0, c).wait_recv()

            for z in range(ZN):
                first = PAD + c * CR + z
                stack = jnp.concatenate(
                    [fbuf[v, pl.ds(first, YC, stride=ZN), :] for v in range(V)], axis=0
                )
                high = stack.astype(BF16)
                low = (stack - high.astype(F32)).astype(BF16)
                reacted = (
                    jnp.dot(kmat[0], high, preferred_element_type=F32)
                    + jnp.dot(kmat[0], low, preferred_element_type=F32)
                    + jnp.dot(kmat[1], high, preferred_element_type=F32)
                )
                rfb[...] = reacted.reshape(V, YC, XN)
                scale = 0.125 * time_step
                vx, vy, vz = (scale * vbuf[d, pl.ds(c * CR + z, YC, stride=ZN), :] for d in range(3))
                faces = xcomb[pl.ds(c * YC, YC), :]

                def variable(v, inner):
                    here = fbuf[v, pl.ds(first, YC, stride=ZN), :]
                    y_plus = fbuf[v, pl.ds(first + ZN, YC, stride=ZN), :]
                    y_minus = fbuf[v, pl.ds(first - ZN, YC, stride=ZN), :]
                    if z < ZN - 1:
                        z_plus = fbuf[v, pl.ds(first + 1, YC, stride=ZN), :]
                    else:
                        z_plus = zrecv[1, c, v].astype(F32)
                    if z > 0:
                        z_minus = fbuf[v, pl.ds(first - 1, YC, stride=ZN), :]
                    else:
                        z_minus = zrecv[0, c, v].astype(F32)
                    at = 2 * (v * ZN + z)
                    moved = pltpu.roll(faces, XN - 1 - at, 1)
                    x_plus = pltpu.roll(jnp.where(edge == 0, moved, here), XN - 1, 1)
                    x_minus = pltpu.roll(jnp.where(edge == XN - 1, moved, here), 1, 1)
                    laplace = (
                        (x_plus + x_minus) + (y_plus + y_minus) + (z_plus + z_minus) - 6.0 * here
                    )
                    advection = (
                        vx * (x_plus - x_minus) + vy * (y_plus - y_minus) + vz * (z_plus - z_minus)
                    )
                    began = sbuf[v, pl.ds(c * CR + z, YC, stride=ZN), :]
                    value = (
                        0.75 * began + 0.25 * here
                        + ((0.25 * time_step) * dif[v]) * laplace - advection + rfb[v]
                    )
                    obuf[v, pl.ds(c * CR + z, YC, stride=ZN), :] = value
                    snap[c, z, v] = value.astype(BF16)
                    return inner

                lax.fori_loop(0, V, variable, 0, unroll=True)
            hand_over(c)
            return carry

        lax.fori_loop(0, NC, chunk, 0)

    diagonal = gy == ga
    diagonal_device = (ga, gz, ga)

    def project_copy(c):
        return bring(
            pbuf.at[c], mbuf.at[:, gy * NC + c], ps_sem.at[c], pr_sem.at[gy * NC + c], diagonal_device
        )

    zero = jnp.zeros_like(xft[...])
    first_half = jnp.concatenate([xft[...], zero], axis=0)
    second_half = jnp.concatenate([zero, xft[...]], axis=0)
    nt = (((1,), (1,)), ((), ()))
    tn = (((0,), (0,)), ((), ()))

    def gather_gram(c, carry):
        for j in range(1, NA):
            arrived(c, j).wait_recv()
        wide = jnp.concatenate([full[c, s].reshape(V * YC, XN) for s in range(NA)], axis=1)
        for i in range(2):
            half = (core + 1 + i) % 2
            part = jnp.concatenate(
                [full[c, 2 * half + s].reshape(V * YC, XN) for s in range(2)], axis=1
            )
            term = lax.dot_general(wide, part, tn, preferred_element_type=F32)

            @pl.when(c == 0)
            def _():
                gacc[i] = term

            @pl.when(c > 0)
            def _():
                gacc[i] = gacc[i] + term

            if i == 0:
                @pl.when(c == NC - 1)
                def _():
                    bring(gacc.at[0], r1, s1_sem, r1_sem, (gy, gz, zhi * 2 + 1 - core)).start()

        rows = V * YC // 2
        projected = lax.dot_general(wide[:rows], first_half, nt, preferred_element_type=F32)
        projected += lax.dot_general(wide[rows:], second_half, nt, preferred_element_type=F32)
        projected = projected.astype(BF16).reshape(V // 2, YC, XN)

        @pl.when(diagonal)
        def _():
            mbuf[:, gy * NC + c] = projected

        @pl.when(jnp.logical_not(diagonal))
        def _():
            pbuf[c] = projected
            project_copy(c).start()

        return carry

    lax.fori_loop(0, NC, gather_gram, 0)

    pair = bring(gacc.at[0], r1, s1_sem, r1_sem, (gy, gz, zhi * 2 + 1 - core))
    pair.wait_recv()
    g2[...] = (gacc[1] + r1[...]).astype(BF16).reshape(16, 32, 256)

    def plane_copy(j):
        to = (plane + j) % 16
        return bring(g2.at[to], r2.at[plane], s2_sem.at[j], r2_sem.at[plane], plane_device(to))

    def plane_arrived(j):
        source = (plane + j) % 16
        return bring(g2.at[source], r2.at[source], s2_sem.at[j], r2_sem.at[source], plane_device(source))

    def start_plane(j, carry):
        plane_copy(j).start()
        return carry

    lax.fori_loop(1, 16, start_plane, 0)

    def bcast_copy(j):
        peer = (ga + j) % NA
        return bring(ysend, yrecv, bs_sem.at[j], br_sem, (gy, gz, peer))

    @pl.when(diagonal)
    def _():
        def wait_projected(i, carry):
            slot = (gy * NC + NC + i) % 16
            bring(
                pbuf.at[0], mbuf.at[:, slot], ps_sem.at[0], pr_sem.at[slot], diagonal_device
            ).wait_recv()
            return carry

        lax.fori_loop(0, 3 * NC, wait_projected, 0)
        y_gram = jnp.zeros((256, 256), F32)
        for i in range(V // 2):
            layer = mbuf[i].reshape(256, XN)
            y_gram += lax.dot_general(layer, layer, nt, preferred_element_type=F32)
        product = jnp.dot(
            yft[...], y_gram * (1.0 / 1024.0), precision=lax.Precision.HIGHEST, preferred_element_type=F32
        )
        ysend[...] = product
        yprod_out[...] = product
        for j in (2, 3, 1):
            bcast_copy(j).start()

    def add_plane(j, acc):
        plane_arrived(j).wait_recv()
        return acc + r2[(plane + j) % 16].astype(F32)

    total = lax.fori_loop(1, 16, add_plane, g2[plane].astype(F32))
    s2[...] = total.reshape(4, 8, 256)
    r3[column] = s2[cz]

    def column_copy(j):
        to = (column + j) % 16
        return bring(s2.at[(to // 2) % 4], r3.at[column], s3_sem.at[j], r3_sem.at[column], column_device(to))

    def column_arrived(j):
        source = (column + j) % 16
        return bring(s2.at[0], r3.at[source], s3_sem.at[j], r3_sem.at[source], column_device(source))

    def start_column(j, carry):
        column_copy(j).start()
        return carry

    lax.fori_loop(1, 16, start_column, 0)

    @pl.when(low_z)
    def _():
        for c in range(NC):
            z_copy(0, c).wait_send()

    @pl.when(high_z)
    def _():
        for c in range(NC):
            z_copy(1, c).wait_send()

    @pl.when(low_y)
    def _():
        y_copy(0).wait_send()

    @pl.when(high_y)
    def _():
        y_copy(1).wait_send()

    @pl.when(low_x)
    def _():
        x_copy(0).wait_send()

    @pl.when(high_x)
    def _():
        x_copy(1).wait_send()

    def sent(c, carry):
        for j in range(1, NA):
            exchange(c, j).wait_send()
        store_out(c).wait()

        @pl.when(jnp.logical_not(diagonal))
        def _():
            project_copy(c).wait_send()

        return carry

    lax.fori_loop(0, NC, sent, 0)
    pair.wait_send()

    def plane_sent(j, carry):
        plane_copy(j).wait_send()
        return carry

    lax.fori_loop(1, 16, plane_sent, 0)

    @pl.when(diagonal)
    def _():
        for j in range(1, NA):
            bcast_copy(j).wait_send()

    @pl.when(jnp.logical_not(diagonal))
    def _():
        bcast_copy(1).wait_recv()
        yprod_out[...] = yrecv[...]

    def column_wait(j, carry):
        column_arrived(j).wait_recv()
        return carry

    lax.fori_loop(1, 16, column_wait, 0)
    cells = 1.0 / float(V * 256 * 64)
    for half in range(2):
        acc = r3[half]
        for z in range(1, 8):
            acc = acc + r3[2 * z + half]
        gram_out[:, 256 * half : 256 * (half + 1)] = acc * cells

    def column_sent(j, carry):
        column_copy(j).wait_send()
        return carry

    lax.fori_loop(1, 16, column_sent, 0)


def shards(fields, section_start, velocity, diffusivity, reaction, x_factor, y_factor):
    vmem = pl.BlockSpec(memory_space=pltpu.VMEM)
    hbm = pl.BlockSpec(memory_space=pl.ANY)
    dma = pltpu.SemaphoreType.DMA
    new_fields, gram, product = pl.pallas_call(
        kernel,
        out_shape=(
            jax.ShapeDtypeStruct((V, ROWS, XN), F32),
            jax.ShapeDtypeStruct((8, 512), F32),
            jax.ShapeDtypeStruct((64, 256), F32),
        ),
        in_specs=[pl.BlockSpec(memory_space=pltpu.SMEM), vmem, vmem, vmem, hbm, hbm, hbm],
        out_specs=(hbm, vmem, vmem),
        scratch_shapes=[
            pltpu.VMEM((V, PAD + ROWS + PAD, XN), F32),
            pltpu.VMEM((V, ROWS, XN), F32),
            pltpu.VMEM((3, ROWS, XN), F32),
            pltpu.VMEM((V, ROWS, XN), F32),
            pltpu.VMEM((2, NC, V, YC, XN), BF16),
            pltpu.VMEM((2, NC, V, YC, XN), BF16),
            pltpu.VMEM((YN, XN), F32),
            pltpu.VMEM((2, YN, XN), F32),
            pltpu.VMEM((YN, XN), F32),
            pltpu.VMEM((NC, ZN, V, YC, XN), BF16),
            pltpu.VMEM((NC, NA, V, YC, XN), BF16),
            pltpu.VMEM((2, V * YC, V * YC), BF16),
            pltpu.VMEM((V, YC, XN), F32),
            pltpu.VMEM((2, 512, 256), F32),
            pltpu.VMEM((512, 256), F32),
            pltpu.VMEM((16, 32, 256), BF16),
            pltpu.VMEM((16, 32, 256), BF16),
            pltpu.VMEM((4, 8, 256), F32),
            pltpu.VMEM((16, 8, 256), F32),
            pltpu.VMEM((NC, V // 2, YC, XN), BF16),
            pltpu.VMEM((V // 2, 16, YC, XN), BF16),
            pltpu.VMEM((64, 256), F32),
            pltpu.VMEM((64, 256), F32),
            dma((3,)), dma((NC,)),
            dma((2, NC)), dma((2, NC)), dma((2,)), dma((2,)), dma((2,)), dma((2,)),
            dma((NC, NA)), dma((NC, NA)),
            dma((NC,)), dma((16,)), dma((NA,)), dma,
            dma, dma, dma((16,)), dma((16,)), dma((16,)), dma((16,)),
        ],
        compiler_params=pltpu.CompilerParams(
            collective_id=0, has_side_effects=True, vmem_limit_bytes=40 << 20
        ),
        name="section",
    )(
        diffusivity,
        reaction,
        x_factor.T,
        y_factor.T,
        fields.reshape(V, ROWS, XN),
        section_start.reshape(V, ROWS, XN),
        velocity.reshape(3, ROWS, XN),
    )
    return new_fields.reshape(V, YN, ZN, XN), gram, product.T[None]


def solution(mesh):
    in_specs = (
        P(None, "gy", "gz", "ga"),
        P(None, "gy", "gz", "ga"),
        P(None, "gy", "gz", "ga"),
        P(),
        P(),
        P(),
        P(),
    )
    out_specs = (P(None, "gy", "gz", "ga"), P(("gy", "gz"), None), P(("gz", "gy"), None, None))
    return jax.shard_map(shards, mesh=mesh, in_specs=in_specs, out_specs=out_specs, check_vma=False)
```

```python
import functools

import jax
import jax.numpy as jnp
from jax import lax
from jax.experimental import pallas as pl
from jax.experimental.pallas import tpu as pltpu
from jax.sharding import PartitionSpec as P

time_step = 0.4

MESH = pl.DeviceIdType.MESH
V = 16
YN = 64
ZN = 4
XN = 128
ROWS = YN * ZN
NC = 4
YC = YN // NC
CR = YC * ZN
PAD = 8
NY, NZ, NA = 4, 16, 4
F32, BF16 = jnp.float32, jnp.bfloat16


def bring(src, dst, send_sem, recv_sem, device):
    return pltpu.make_async_remote_copy(
        src_ref=src, dst_ref=dst, send_sem=send_sem, recv_sem=recv_sem, device_id=device, device_id_type=MESH
    )


def kernel(
    dif_in, rea_in, xft_in, yft_in, fields, start, vel,
    new_out, gram_out, yprod_out,
    dif, rea, xft, yft, fbuf, sbuf, vbuf, zsend, zrecv, xpack, xrecv, xcomb, snap, full, kmat, rfb,
    gacc, r1, g2, r2, s2, r3, pbuf, mbuf, ysend, yrecv,
    load_sem, zs_sem, zr_sem, ys_sem, yr_sem, xs_sem, xr_sem, as_sem, ar_sem,
    ps_sem, pr_sem, bs_sem, br_sem, s1_sem, r1_sem, s2_sem, r2_sem, s3_sem, r3_sem,
):
    gy, gz, ga = lax.axis_index("gy"), lax.axis_index("gz"), lax.axis_index("ga")
    cy, cz = gz // 4, gz % 4
    zhi, core = ga // 2, ga % 2
    plane = gy * 4 + cy
    column = (zhi * 4 + cz) * 2 + core
    buffer_slab = ga == NA - 1
    inner_slab = ga < NA - 1

    def plane_device(index):
        return (index // 4, (index % 4) * 4 + cz, ga)

    def column_device(index):
        return (gy, cy * 4 + (index // 2) % 4, (index // 8) * 2 + index % 2)

    load_f = pltpu.make_async_copy(fields, fbuf.at[:, pl.ds(PAD, ROWS), :], load_sem.at[0])
    load_s = pltpu.make_async_copy(start, sbuf, load_sem.at[1])
    load_v = pltpu.make_async_copy(vel, vbuf, load_sem.at[2])
    load_small = [
        pltpu.make_async_copy(src, dst, load_sem.at[3 + i])
        for i, (src, dst) in enumerate(((rea_in, rea), (dif_in, dif), (xft_in, xft), (yft_in, yft)))
    ]
    load_f.start()
    load_small[0].start()
    load_s.start()
    load_v.start()
    for copy in load_small[1:]:
        copy.start()

    barrier = pltpu.get_barrier_semaphore()
    wrap_up = jnp.logical_and(cz == 3, gz < NZ - 1)
    wrap_down = jnp.logical_and(cz == 0, gz > 0)

    @pl.when(wrap_up)
    def _():
        pl.semaphore_signal(barrier, inc=1, device_id=(gy, gz + 1, ga), device_id_type=MESH)

    @pl.when(wrap_down)
    def _():
        pl.semaphore_signal(barrier, inc=1, device_id=(gy, gz - 1, ga), device_id_type=MESH)

    def greet(j, carry):
        pl.semaphore_signal(barrier, inc=1, device_id=plane_device((plane + j) % 16), device_id_type=MESH)
        pl.semaphore_signal(barrier, inc=1, device_id=column_device((column + j) % 16), device_id_type=MESH)
        return carry

    lax.fori_loop(1, 16, greet, 0)

    @pl.when(gy == 0)
    def _():
        fbuf[:, 0:PAD, :] = jnp.zeros((V, PAD, XN), F32)

    @pl.when(gy == NY - 1)
    def _():
        fbuf[:, PAD + ROWS : PAD + ROWS + PAD, :] = jnp.zeros((V, PAD, XN), F32)

    @pl.when(gz == 0)
    def _():
        zrecv[0] = jnp.zeros((NC, V, YC, XN), BF16)

    @pl.when(gz == NZ - 1)
    def _():
        zrecv[1] = jnp.zeros((NC, V, YC, XN), BF16)

    @pl.when(ga == 0)
    def _():
        xrecv[0] = jnp.zeros((YN, XN), F32)

    load_small[0].wait()

    low16 = lax.broadcasted_iota(jnp.int32, (V * YC, V), 0) // YC
    spread = (low16 == lax.broadcasted_iota(jnp.int32, (V * YC, V), 1)).astype(F32).astype(BF16)
    rows_at = lax.broadcasted_iota(jnp.int32, (V * YC, V * YC), 0) % YC
    cols_at = lax.broadcasted_iota(jnp.int32, (V * YC, V * YC), 1) % YC
    same = rows_at == cols_at
    rate = (0.25 * time_step) * rea[...]
    rate_high = rate.astype(BF16)
    rate_low = (rate - rate_high.astype(F32)).astype(BF16)
    for part, piece in enumerate((rate_high, rate_low)):
        tall = jnp.dot(spread, piece, preferred_element_type=F32).astype(BF16)
        square = lax.dot_general(tall, spread, (((1,), (1,)), ((), ())), preferred_element_type=F32)
        kmat[part] = jnp.where(same, square, 0.0).astype(BF16)

    load_f.wait()

    @pl.when(inner_slab)
    def _():
        def face(v, carry):
            for side, z in ((0, 0), (1, ZN - 1)):
                for c in range(NC):
                    piece = fbuf[v, pl.ds(PAD + c * CR + z, YC, stride=ZN), :]
                    zsend[side, c, v] = piece.astype(BF16)
            return carry

        lax.fori_loop(0, V, face, 0)

    pl.semaphore_wait(barrier, 30 + wrap_up.astype(jnp.int32) + wrap_down.astype(jnp.int32))

    def z_copy(side, c):
        return bring(
            zsend.at[side, c], zrecv.at[1 - side, c], zs_sem.at[side, c], zr_sem.at[1 - side, c],
            (gy, gz - 1 + 2 * side, ga),
        )

    low_z = jnp.logical_and(inner_slab, gz > 0)
    high_z = jnp.logical_and(inner_slab, gz < NZ - 1)
    low_y = jnp.logical_and(inner_slab, gy > 0)
    high_y = jnp.logical_and(inner_slab, gy < NY - 1)

    def y_copy(side):
        src = fields.at[:, pl.ds((ROWS - PAD) * side, PAD), :]
        dst = fbuf.at[:, pl.ds((PAD + ROWS) * (1 - side), PAD), :]
        return bring(src, dst, ys_sem.at[side], yr_sem.at[1 - side], (gy - 1 + 2 * side, gz, ga))

    for c in range(NC):
        @pl.when(low_z)
        def _():
            z_copy(0, c).start()

        @pl.when(high_z)
        def _():
            z_copy(1, c).start()

        if c == 0:
            @pl.when(low_y)
            def _():
                y_copy(0).start()

            @pl.when(high_y)
            def _():
                y_copy(1).start()

    lane = lax.broadcasted_iota(jnp.int32, (YN, XN), 1)

    def pack(v, acc):
        for z in range(ZN):
            at = 2 * (v * ZN + z)
            piece = fbuf[v, pl.ds(PAD + z, YN, stride=ZN), :]
            moved = pltpu.roll(piece, at + 1, 1)
            acc = jnp.where(jnp.logical_or(lane == at, lane == at + 1), moved, acc)
        return acc

    xpack[...] = lax.fori_loop(0, V, pack, jnp.zeros((YN, XN), F32))

    def x_copy(side):
        return bring(
            xpack, xrecv.at[1 - side], xs_sem.at[side], xr_sem.at[1 - side], (gy, gz, ga - 1 + 2 * side)
        )

    low_x = ga > 0
    high_x = ga < NA - 2

    @pl.when(low_x)
    def _():
        x_copy(0).start()

    @pl.when(high_x)
    def _():
        x_copy(1).start()

    def exchange(c, j):
        peer = (ga + j) % NA
        return bring(snap.at[c, peer], full.at[c, ga], as_sem.at[c, j], ar_sem.at[c, ga], (gy, gz, peer))

    def arrived(c, j):
        slab = (ga + j) % NA
        return bring(snap.at[c, slab], full.at[c, slab], as_sem.at[c, j], ar_sem.at[c, slab], (gy, gz, slab))

    def hand_over(c):
        full[c, ga] = snap[c, ga]
        for j in (2, 3, 1):
            exchange(c, j).start()

    load_s.wait()
    load_v.wait()
    for copy in load_small[1:]:
        copy.wait()

    @pl.when(buffer_slab)
    def _():
        def chunk(c, carry):
            def variable(v, inner):
                new_out[v, pl.ds(c * CR, CR), :] = fbuf[v, pl.ds(PAD + c * CR, CR), :]
                for z in range(ZN):
                    piece = fbuf[v, pl.ds(PAD + c * CR + z, YC, stride=ZN), :]
                    snap[c, z, v] = piece.astype(BF16)
                return inner

            lax.fori_loop(0, V, variable, 0)
            hand_over(c)
            return carry

        lax.fori_loop(0, NC, chunk, 0)

    @pl.when(inner_slab)
    def _():
        @pl.when(gy > 0)
        def _():
            y_copy(1).wait_recv()

        @pl.when(gy < NY - 1)
        def _():
            y_copy(0).wait_recv()

        @pl.when(ga > 0)
        def _():
            x_copy(1).wait_recv()

        x_copy(0).wait_recv()
        xcomb[...] = jnp.where(lane % 2 == 0, xrecv[0], xrecv[1])
        edge = lax.broadcasted_iota(jnp.int32, (YC, XN), 1)

        def chunk(c, carry):
            @pl.when(gz > 0)
            def _():
                z_copy(1, c).wait_recv()

            @pl.when(gz < NZ - 1)
            def _():
                z_copy(0, c).wait_recv()

            for z in range(ZN):
                first = PAD + c * CR + z
                stack = jnp.concatenate(
                    [fbuf[v, pl.ds(first, YC, stride=ZN), :] for v in range(V)], axis=0
                )
                high = stack.astype(BF16)
                low = (stack - high.astype(F32)).astype(BF16)
                reacted = (
                    jnp.dot(kmat[0], high, preferred_element_type=F32)
                    + jnp.dot(kmat[0], low, preferred_element_type=F32)
                    + jnp.dot(kmat[1], high, preferred_element_type=F32)
                )
                rfb[...] = reacted.reshape(V, YC, XN)
                scale = 0.125 * time_step
                vx, vy, vz = (scale * vbuf[d, pl.ds(c * CR + z, YC, stride=ZN), :] for d in range(3))
                faces = xcomb[pl.ds(c * YC, YC), :]

                def variable(v, inner):
                    here = fbuf[v, pl.ds(first, YC, stride=ZN), :]
                    y_plus = fbuf[v, pl.ds(first + ZN, YC, stride=ZN), :]
                    y_minus = fbuf[v, pl.ds(first - ZN, YC, stride=ZN), :]
                    if z < ZN - 1:
                        z_plus = fbuf[v, pl.ds(first + 1, YC, stride=ZN), :]
                    else:
                        z_plus = zrecv[1, c, v].astype(F32)
                    if z > 0:
                        z_minus = fbuf[v, pl.ds(first - 1, YC, stride=ZN), :]
                    else:
                        z_minus = zrecv[0, c, v].astype(F32)
                    at = 2 * (v * ZN + z)
                    moved = pltpu.roll(faces, XN - 1 - at, 1)
                    x_plus = pltpu.roll(jnp.where(edge == 0, moved, here), XN - 1, 1)
                    x_minus = pltpu.roll(jnp.where(edge == XN - 1, moved, here), 1, 1)
                    laplace = (
                        (x_plus + x_minus) + (y_plus + y_minus) + (z_plus + z_minus) - 6.0 * here
                    )
                    advection = (
                        vx * (x_plus - x_minus) + vy * (y_plus - y_minus) + vz * (z_plus - z_minus)
                    )
                    began = sbuf[v, pl.ds(c * CR + z, YC, stride=ZN), :]
                    value = (
                        0.75 * began + 0.25 * here
                        + ((0.25 * time_step) * dif[v]) * laplace - advection + rfb[v]
                    )
                    new_out[v, pl.ds(c * CR + z, YC, stride=ZN), :] = value
                    snap[c, z, v] = value.astype(BF16)
                    return inner

                lax.fori_loop(0, V, variable, 0, unroll=True)
            hand_over(c)
            return carry

        lax.fori_loop(0, NC, chunk, 0)

    diagonal = gy == ga
    diagonal_device = (ga, gz, ga)

    def project_copy(c):
        return bring(
            pbuf.at[c], mbuf.at[:, gy * NC + c], ps_sem.at[c], pr_sem.at[gy * NC + c], diagonal_device
        )

    zero = jnp.zeros_like(xft[...])
    first_half = jnp.concatenate([xft[...], zero], axis=0)
    second_half = jnp.concatenate([zero, xft[...]], axis=0)
    nt = (((1,), (1,)), ((), ()))
    tn = (((0,), (0,)), ((), ()))

    def gather_gram(c, carry):
        for j in range(1, NA):
            arrived(c, j).wait_recv()
        wide = jnp.concatenate([full[c, s].reshape(V * YC, XN) for s in range(NA)], axis=1)
        for i in range(2):
            half = (core + 1 + i) % 2
            part = jnp.concatenate(
                [full[c, 2 * half + s].reshape(V * YC, XN) for s in range(2)], axis=1
            )
            term = lax.dot_general(wide, part, tn, preferred_element_type=F32)

            @pl.when(c == 0)
            def _():
                gacc[i] = term

            @pl.when(c > 0)
            def _():
                gacc[i] = gacc[i] + term

            if i == 0:
                @pl.when(c == NC - 1)
                def _():
                    bring(gacc.at[0], r1, s1_sem, r1_sem, (gy, gz, zhi * 2 + 1 - core)).start()

        rows = V * YC // 2
        projected = lax.dot_general(wide[:rows], first_half, nt, preferred_element_type=F32)
        projected += lax.dot_general(wide[rows:], second_half, nt, preferred_element_type=F32)
        projected = projected.astype(BF16).reshape(V // 2, YC, XN)

        @pl.when(diagonal)
        def _():
            mbuf[:, gy * NC + c] = projected

        @pl.when(jnp.logical_not(diagonal))
        def _():
            pbuf[c] = projected
            project_copy(c).start()

        return carry

    lax.fori_loop(0, NC, gather_gram, 0)

    pair = bring(gacc.at[0], r1, s1_sem, r1_sem, (gy, gz, zhi * 2 + 1 - core))
    pair.wait_recv()
    g2[...] = (gacc[1] + r1[...]).astype(BF16).reshape(16, 32, 256)

    def plane_copy(j):
        to = (plane + j) % 16
        return bring(g2.at[to], r2.at[plane], s2_sem.at[j], r2_sem.at[plane], plane_device(to))

    def plane_arrived(j):
        source = (plane + j) % 16
        return bring(g2.at[source], r2.at[source], s2_sem.at[j], r2_sem.at[source], plane_device(source))

    def start_plane(j, carry):
        plane_copy(j).start()
        return carry

    lax.fori_loop(1, 16, start_plane, 0)

    def bcast_copy(j):
        peer = (ga + j) % NA
        return bring(ysend, yrecv, bs_sem.at[j], br_sem, (gy, gz, peer))

    @pl.when(diagonal)
    def _():
        def wait_projected(i, carry):
            slot = (gy * NC + NC + i) % 16
            bring(
                pbuf.at[0], mbuf.at[:, slot], ps_sem.at[0], pr_sem.at[slot], diagonal_device
            ).wait_recv()
            return carry

        lax.fori_loop(0, 3 * NC, wait_projected, 0)
        y_gram = jnp.zeros((256, 256), F32)
        for i in range(V // 2):
            layer = mbuf[i].reshape(256, XN)
            y_gram += lax.dot_general(layer, layer, nt, preferred_element_type=F32)
        product = jnp.dot(
            yft[...], y_gram * (1.0 / 1024.0), precision=lax.Precision.HIGHEST, preferred_element_type=F32
        )
        ysend[...] = product
        yprod_out[...] = product
        for j in (2, 3, 1):
            bcast_copy(j).start()

    def add_plane(j, acc):
        plane_arrived(j).wait_recv()
        return acc + r2[(plane + j) % 16].astype(F32)

    total = lax.fori_loop(1, 16, add_plane, g2[plane].astype(F32))
    s2[...] = total.reshape(4, 8, 256)
    r3[column] = s2[cz]

    def column_copy(j):
        to = (column + j) % 16
        return bring(s2.at[(to // 2) % 4], r3.at[column], s3_sem.at[j], r3_sem.at[column], column_device(to))

    def column_arrived(j):
        source = (column + j) % 16
        return bring(s2.at[0], r3.at[source], s3_sem.at[j], r3_sem.at[source], column_device(source))

    def start_column(j, carry):
        column_copy(j).start()
        return carry

    lax.fori_loop(1, 16, start_column, 0)

    @pl.when(low_z)
    def _():
        for c in range(NC):
            z_copy(0, c).wait_send()

    @pl.when(high_z)
    def _():
        for c in range(NC):
            z_copy(1, c).wait_send()

    @pl.when(low_y)
    def _():
        y_copy(0).wait_send()

    @pl.when(high_y)
    def _():
        y_copy(1).wait_send()

    @pl.when(low_x)
    def _():
        x_copy(0).wait_send()

    @pl.when(high_x)
    def _():
        x_copy(1).wait_send()

    def sent(c, carry):
        for j in range(1, NA):
            exchange(c, j).wait_send()

        @pl.when(jnp.logical_not(diagonal))
        def _():
            project_copy(c).wait_send()

        return carry

    lax.fori_loop(0, NC, sent, 0)
    pair.wait_send()

    def plane_sent(j, carry):
        plane_copy(j).wait_send()
        return carry

    lax.fori_loop(1, 16, plane_sent, 0)

    @pl.when(diagonal)
    def _():
        for j in range(1, NA):
            bcast_copy(j).wait_send()

    @pl.when(jnp.logical_not(diagonal))
    def _():
        bcast_copy(1).wait_recv()
        yprod_out[...] = yrecv[...]

    def column_wait(j, carry):
        column_arrived(j).wait_recv()
        return carry

    lax.fori_loop(1, 16, column_wait, 0)
    cells = 1.0 / float(V * 256 * 64)
    for half in range(2):
        acc = r3[half]
        for z in range(1, 8):
            acc = acc + r3[2 * z + half]
        gram_out[:, 256 * half : 256 * (half + 1)] = acc * cells

    def column_sent(j, carry):
        column_copy(j).wait_send()
        return carry

    lax.fori_loop(1, 16, column_sent, 0)


def finish(new, gram, product, new_out, gram_out, product_out, sem):
    copies = [
        pltpu.make_async_copy(src, dst, sem.at[i])
        for i, (src, dst) in enumerate(((new, new_out), (gram, gram_out), (product, product_out)))
    ]
    for copy in copies:
        copy.start()
    for copy in copies:
        copy.wait()


def shards(fields, section_start, velocity, diffusivity, reaction, x_factor, y_factor):
    vmem = pl.BlockSpec(memory_space=pltpu.VMEM)
    hbm = pl.BlockSpec(memory_space=pltpu.HBM)
    dma = pltpu.SemaphoreType.DMA
    new_fields, gram, product = pl.pallas_call(
        kernel,
        out_shape=(
            pltpu.VMEM((V, ROWS, XN), F32),
            pltpu.VMEM((8, 512), F32),
            pltpu.VMEM((64, 256), F32),
        ),
        in_specs=[hbm] * 7,
        out_specs=(vmem, vmem, vmem),
        scratch_shapes=[
            pltpu.SMEM((V,), F32),
            pltpu.VMEM((V, V), F32),
            pltpu.VMEM((64, 512), BF16),
            pltpu.VMEM((64, 256), F32),
            pltpu.VMEM((V, PAD + ROWS + PAD, XN), F32),
            pltpu.VMEM((V, ROWS, XN), F32),
            pltpu.VMEM((3, ROWS, XN), F32),
            pltpu.VMEM((2, NC, V, YC, XN), BF16),
            pltpu.VMEM((2, NC, V, YC, XN), BF16),
            pltpu.VMEM((YN, XN), F32),
            pltpu.VMEM((2, YN, XN), F32),
            pltpu.VMEM((YN, XN), F32),
            pltpu.VMEM((NC, ZN, V, YC, XN), BF16),
            pltpu.VMEM((NC, NA, V, YC, XN), BF16),
            pltpu.VMEM((2, V * YC, V * YC), BF16),
            pltpu.VMEM((V, YC, XN), F32),
            pltpu.VMEM((2, 512, 256), F32),
            pltpu.VMEM((512, 256), F32),
            pltpu.VMEM((16, 32, 256), BF16),
            pltpu.VMEM((16, 32, 256), BF16),
            pltpu.VMEM((4, 8, 256), F32),
            pltpu.VMEM((16, 8, 256), F32),
            pltpu.VMEM((NC, V // 2, YC, XN), BF16),
            pltpu.VMEM((V // 2, 16, YC, XN), BF16),
            pltpu.VMEM((64, 256), F32),
            pltpu.VMEM((64, 256), F32),
            dma((7,)),
            dma((2, NC)), dma((2, NC)), dma((2,)), dma((2,)), dma((2,)), dma((2,)),
            dma((NC, NA)), dma((NC, NA)),
            dma((NC,)), dma((16,)), dma((NA,)), dma,
            dma, dma, dma((16,)), dma((16,)), dma((16,)), dma((16,)),
        ],
        compiler_params=pltpu.CompilerParams(
            collective_id=0, has_side_effects=True, vmem_limit_bytes=24 << 20
        ),
        name="section",
    )(
        *(
            pltpu.with_memory_space_constraint(array, pltpu.HBM)
            for array in (
                diffusivity,
                reaction,
                x_factor.T,
                y_factor.T,
                fields.reshape(V, ROWS, XN),
                section_start.reshape(V, ROWS, XN),
                velocity.reshape(3, ROWS, XN),
            )
        )
    )
    new_fields, gram, product = pl.pallas_call(
        finish,
        out_shape=(
            jax.ShapeDtypeStruct((V, ROWS, XN), F32),
            jax.ShapeDtypeStruct((8, 512), F32),
            jax.ShapeDtypeStruct((64, 256), F32),
        ),
        in_specs=[pl.BlockSpec(memory_space=pl.ANY)] * 3,
        out_specs=(hbm,) * 3,
        scratch_shapes=[dma((3,))],
        name="finish", compiler_params=pltpu.CompilerParams(vmem_limit_bytes=1 << 20),
    )(new_fields, gram, product)
    return new_fields.reshape(V, YN, ZN, XN), gram, product.T[None]


def solution(mesh):
    in_specs = (
        P(None, "gy", "gz", "ga"),
        P(None, "gy", "gz", "ga"),
        P(None, "gy", "gz", "ga"),
        P(),
        P(),
        P(),
        P(),
    )
    out_specs = (P(None, "gy", "gz", "ga"), P(("gy", "gz"), None), P(("gz", "gy"), None, None))
    return jax.shard_map(shards, mesh=mesh, in_specs=in_specs, out_specs=out_specs, check_vma=False)
```

```python
import functools

import jax
import jax.numpy as jnp
from jax import lax
from jax.experimental import pallas as pl
from jax.experimental.pallas import tpu as pltpu
from jax.sharding import PartitionSpec as P

time_step = 0.4

MESH = pl.DeviceIdType.MESH
V = 16
YN = 64
ZN = 4
XN = 128
ROWS = YN * ZN
NC = 4
YC = YN // NC
CR = YC * ZN
PAD = 8
NY, NZ, NA = 4, 16, 4
F32, BF16 = jnp.float32, jnp.bfloat16


def bring(src, dst, send_sem, recv_sem, device):
    return pltpu.make_async_remote_copy(
        src_ref=src, dst_ref=dst, send_sem=send_sem, recv_sem=recv_sem, device_id=device, device_id_type=MESH
    )


def kernel(
    dif_in, rea_in, xft_in, yft_in, fields, start, vel,
    new_out, gram_out, yprod_out,
    dif, rea, xft, yft, fbuf, sbuf, vbuf, zsend, zrecv, xpack, xrecv, xcomb, snap, full, kmat, rfb,
    gacc, r1, g2, r2, s2, r3, pbuf, mbuf, ysend, yrecv,
    load_sem, zs_sem, zr_sem, ys_sem, yr_sem, xs_sem, xr_sem, as_sem, ar_sem,
    ps_sem, pr_sem, bs_sem, br_sem, s1_sem, r1_sem, s2_sem, r2_sem, s3_sem, r3_sem,
):
    gy, gz, ga = lax.axis_index("gy"), lax.axis_index("gz"), lax.axis_index("ga")
    cy, cz = gz // 4, gz % 4
    zhi, core = ga // 2, ga % 2
    plane = gy * 4 + cy
    column = (zhi * 4 + cz) * 2 + core
    buffer_slab = ga == NA - 1
    first_chip = zhi == 0
    second_chip = zhi == 1
    diagonal = gy == ga
    to_second = jnp.logical_and(first_chip, gy != ga + 2)
    from_first = jnp.logical_and(second_chip, diagonal)
    inner_slab = ga < NA - 1

    def plane_device(index):
        return (index // 4, (index % 4) * 4 + cz, ga)

    def column_device(index):
        return (gy, cy * 4 + (index // 2) % 4, (index // 8) * 2 + index % 2)

    load_f = pltpu.make_async_copy(fields, fbuf.at[:, pl.ds(PAD, ROWS), :], load_sem.at[0])
    load_s = pltpu.make_async_copy(start, sbuf, load_sem.at[1])
    load_v = pltpu.make_async_copy(vel, vbuf, load_sem.at[2])
    load_small = [
        pltpu.make_async_copy(src, dst, load_sem.at[3 + i])
        for i, (src, dst) in enumerate(((rea_in, rea), (dif_in, dif), (xft_in, xft), (yft_in, yft)))
    ]
    load_f.start()
    load_small[0].start()
    load_s.start()
    load_v.start()
    for copy in load_small[1:]:
        copy.start()

    barrier = pltpu.get_barrier_semaphore()
    wrap_up = jnp.logical_and(cz == 3, gz < NZ - 1)
    wrap_down = jnp.logical_and(cz == 0, gz > 0)

    @pl.when(wrap_up)
    def _():
        pl.semaphore_signal(barrier, inc=1, device_id=(gy, gz + 1, ga), device_id_type=MESH)

    @pl.when(wrap_down)
    def _():
        pl.semaphore_signal(barrier, inc=1, device_id=(gy, gz - 1, ga), device_id_type=MESH)

    def greet(j, carry):
        pl.semaphore_signal(barrier, inc=1, device_id=plane_device((plane + j) % 16), device_id_type=MESH)
        pl.semaphore_signal(barrier, inc=1, device_id=column_device((column + j) % 16), device_id_type=MESH)
        return carry

    for j in range(1, 16):
        greet(j, 0)

    @pl.when(to_second)
    def _():
        pl.semaphore_signal(barrier, inc=1, device_id=(ga + 2, gz, ga + 2), device_id_type=MESH)

    @pl.when(from_first)
    def _():
        for j in range(1, NY):
            pl.semaphore_signal(barrier, inc=1, device_id=((gy + j) % NY, gz, ga - 2), device_id_type=MESH)

    @pl.when(gy == 0)
    def _():
        fbuf[:, 0:PAD, :] = jnp.zeros((V, PAD, XN), F32)

    @pl.when(gy == NY - 1)
    def _():
        fbuf[:, PAD + ROWS : PAD + ROWS + PAD, :] = jnp.zeros((V, PAD, XN), F32)

    @pl.when(gz == 0)
    def _():
        zrecv[0] = jnp.zeros((NC, V, YC, XN), BF16)

    @pl.when(gz == NZ - 1)
    def _():
        zrecv[1] = jnp.zeros((NC, V, YC, XN), BF16)

    @pl.when(ga == 0)
    def _():
        xrecv[0] = jnp.zeros((YN, XN), F32)

    load_f.wait()

    @pl.when(inner_slab)
    def _():
        def face(v, carry):
            for side, z in ((0, 0), (1, ZN - 1)):
                for c in range(NC):
                    piece = fbuf[v, pl.ds(PAD + c * CR + z, YC, stride=ZN), :]
                    zsend[side, c, v] = piece.astype(BF16)
            return carry

        lax.fori_loop(0, V, face, 0)

    pl.semaphore_wait(
        barrier,
        30 + wrap_up.astype(jnp.int32) + wrap_down.astype(jnp.int32)
        + to_second.astype(jnp.int32) + 3 * from_first.astype(jnp.int32),
    )

    def z_copy(side, c):
        return bring(
            zsend.at[side, c], zrecv.at[1 - side, c], zs_sem.at[side, c], zr_sem.at[1 - side, c],
            (gy, gz - 1 + 2 * side, ga),
        )

    low_z = jnp.logical_and(inner_slab, gz > 0)
    high_z = jnp.logical_and(inner_slab, gz < NZ - 1)
    low_y = jnp.logical_and(inner_slab, gy > 0)
    high_y = jnp.logical_and(inner_slab, gy < NY - 1)

    def y_copy(side):
        src = fields.at[:, pl.ds((ROWS - PAD) * side, PAD), :]
        dst = fbuf.at[:, pl.ds((PAD + ROWS) * (1 - side), PAD), :]
        return bring(src, dst, ys_sem.at[side], yr_sem.at[1 - side], (gy - 1 + 2 * side, gz, ga))

    def start_faces(c):
        @pl.when(low_z)
        def _():
            z_copy(0, c).start()

        @pl.when(high_z)
        def _():
            z_copy(1, c).start()

    def faces_sent(c):
        @pl.when(low_z)
        def _():
            z_copy(0, c).wait_send()

        @pl.when(high_z)
        def _():
            z_copy(1, c).wait_send()

    start_faces(0)

    @pl.when(low_y)
    def _():
        y_copy(0).start()

    @pl.when(high_y)
    def _():
        y_copy(1).start()

    lane = lax.broadcasted_iota(jnp.int32, (YN, XN), 1)

    def pack(v, acc):
        for z in range(ZN):
            at = 2 * (v * ZN + z)
            piece = fbuf[v, pl.ds(PAD + z, YN, stride=ZN), :]
            moved = pltpu.roll(piece, at + 1, 1)
            acc = jnp.where(jnp.logical_or(lane == at, lane == at + 1), moved, acc)
        return acc

    xpack[...] = lax.fori_loop(0, V, pack, jnp.zeros((YN, XN), F32))

    def x_copy(side):
        return bring(
            xpack, xrecv.at[1 - side], xs_sem.at[side], xr_sem.at[1 - side], (gy, gz, ga - 1 + 2 * side)
        )

    low_x = ga > 0
    high_x = ga < NA - 2

    @pl.when(low_x)
    def _():
        x_copy(0).start()

    @pl.when(high_x)
    def _():
        x_copy(1).start()

    for c in range(1, NC):
        start_faces(c)

    def exchange(c, j):
        peer = (ga + j) % NA
        return bring(snap.at[c, peer], full.at[c, ga], as_sem.at[c, j], ar_sem.at[c, ga], (gy, gz, peer))

    def arrived(c, j):
        slab = (ga + j) % NA
        return bring(snap.at[c, slab], full.at[c, slab], as_sem.at[c, j], ar_sem.at[c, slab], (gy, gz, slab))

    last = NC - 1

    def last_exchange(layer):
        return bring(
            snap.at[last, layer], full.at[last + layer // 2, ga], as_sem.at[last, layer],
            ar_sem.at[last + layer // 2, ga], (gy, gz, layer % 2),
        )

    def last_swap(m):
        return bring(
            snap.at[last, 2 * m + 1 - core], full.at[last + m, ga], as_sem.at[last, m],
            ar_sem.at[last + m, ga], (gy, gz, 1 - core),
        )

    def last_arrived(block, j):
        slab = (ga + j) % NA
        return bring(
            snap.at[0, slab], full.at[block, slab], as_sem.at[0, j], ar_sem.at[block, slab], (gy, gz, slab)
        )

    def hand_over(c):
        @pl.when(c < last)
        def _():
            full[c, ga] = snap[c, ga]
            for j in (2, 3, 1):
                exchange(c, j).start()

        @pl.when(jnp.logical_and(c == last, first_chip))
        def _():
            for m in range(2):
                last_swap(m).start()
            for m in range(2):
                full[last + m, ga] = snap[last, 2 * m + core]

        @pl.when(jnp.logical_and(c == last, second_chip))
        def _():
            for layer in range(NA):
                last_exchange(layer).start()

    load_small[0].wait()

    low16 = lax.broadcasted_iota(jnp.int32, (V * YC, V), 0) // YC
    spread = (low16 == lax.broadcasted_iota(jnp.int32, (V * YC, V), 1)).astype(F32).astype(BF16)
    rows_at = lax.broadcasted_iota(jnp.int32, (V * YC, V * YC), 0) % YC
    cols_at = lax.broadcasted_iota(jnp.int32, (V * YC, V * YC), 1) % YC
    same = rows_at == cols_at
    rate = (0.25 * time_step) * rea[...]
    rate_high = rate.astype(BF16)
    rate_low = (rate - rate_high.astype(F32)).astype(BF16)
    for part, piece in enumerate((rate_high, rate_high, rate_low)):
        tall = jnp.dot(spread, piece, preferred_element_type=F32).astype(BF16)
        square = lax.dot_general(tall, spread, (((1,), (1,)), ((), ())), preferred_element_type=F32)
        kmat[:, V * YC * part : V * YC * (part + 1)] = jnp.where(same, square, 0.0).astype(BF16)

    load_s.wait()
    load_v.wait()
    for copy in load_small[1:]:
        copy.wait()

    @pl.when(buffer_slab)
    def _():
        def chunk(c, carry):
            def variable(v, inner):
                new_out[v, pl.ds(c * CR, CR), :] = fbuf[v, pl.ds(PAD + c * CR, CR), :]
                for z in range(ZN):
                    piece = fbuf[v, pl.ds(PAD + c * CR + z, YC, stride=ZN), :]
                    snap[c, z, v] = piece.astype(BF16)
                return inner

            lax.fori_loop(0, V, variable, 0)
            hand_over(c)
            return carry

        lax.fori_loop(0, NC, chunk, 0)

    @pl.when(inner_slab)
    def _():
        @pl.when(gy > 0)
        def _():
            y_copy(1).wait_recv()

        @pl.when(gy < NY - 1)
        def _():
            y_copy(0).wait_recv()

        @pl.when(ga > 0)
        def _():
            x_copy(1).wait_recv()

        x_copy(0).wait_recv()
        xcomb[...] = jnp.where(lane % 2 == 0, xrecv[0], xrecv[1])
        edge = lax.broadcasted_iota(jnp.int32, (YC, XN), 1)

        def chunk(c, carry):
            @pl.when(gz > 0)
            def _():
                z_copy(1, c).wait_recv()

            @pl.when(gz < NZ - 1)
            def _():
                z_copy(0, c).wait_recv()

            faces_sent(c)

            for z in range(ZN):
                first = PAD + c * CR + z
                stack = jnp.concatenate(
                    [fbuf[v, pl.ds(first, YC, stride=ZN), :] for v in range(V)], axis=0
                )
                high = stack.astype(BF16)
                low = (stack - high.astype(F32)).astype(BF16)
                reacted = jnp.dot(
                    kmat[...], jnp.concatenate([high, low, high], axis=0), preferred_element_type=F32
                )
                rfb[...] = reacted.reshape(V, YC, XN)
                scale = 0.125 * time_step
                vx, vy, vz = (scale * vbuf[d, pl.ds(c * CR + z, YC, stride=ZN), :] for d in range(3))
                faces = xcomb[pl.ds(c * YC, YC), :]

                def variable(v, inner):
                    here = fbuf[v, pl.ds(first, YC, stride=ZN), :]
                    y_plus = fbuf[v, pl.ds(first + ZN, YC, stride=ZN), :]
                    y_minus = fbuf[v, pl.ds(first - ZN, YC, stride=ZN), :]
                    if z < ZN - 1:
                        z_plus = fbuf[v, pl.ds(first + 1, YC, stride=ZN), :]
                    else:
                        z_plus = zrecv[1, c, v].astype(F32)
                    if z > 0:
                        z_minus = fbuf[v, pl.ds(first - 1, YC, stride=ZN), :]
                    else:
                        z_minus = zrecv[0, c, v].astype(F32)
                    at = 2 * (v * ZN + z)
                    moved = pltpu.roll(faces, XN - 1 - at, 1)
                    x_plus = pltpu.roll(jnp.where(edge == 0, moved, here), XN - 1, 1)
                    x_minus = pltpu.roll(jnp.where(edge == XN - 1, moved, here), 1, 1)
                    laplace = (
                        (x_plus + x_minus) + (y_plus + y_minus) + (z_plus + z_minus) - 6.0 * here
                    )
                    advection = (
                        vx * (x_plus - x_minus) + vy * (y_plus - y_minus) + vz * (z_plus - z_minus)
                    )
                    began = sbuf[v, pl.ds(c * CR + z, YC, stride=ZN), :]
                    value = (
                        0.75 * began + 0.25 * here
                        + ((0.25 * time_step) * dif[v]) * laplace - advection + rfb[v]
                    )
                    new_out[v, pl.ds(c * CR + z, YC, stride=ZN), :] = value
                    snap[c, z, v] = value.astype(BF16)
                    return inner

                lax.fori_loop(0, V, variable, 0, unroll=True)
            hand_over(c)
            return carry

        lax.fori_loop(0, NC, chunk, 0)

    def project_copy(block, layer):
        slot = gy * NC + jnp.minimum(block, last)
        return bring(pbuf.at[block], mbuf.at[:, slot], ps_sem.at[block], pr_sem.at[slot], (layer, gz, layer))

    zero = jnp.zeros_like(xft[...])
    first_half = jnp.concatenate([xft[...], zero], axis=0)
    second_half = jnp.concatenate([zero, xft[...]], axis=0)
    nt = (((1,), (1,)), ((), ()))
    tn = (((0,), (0,)), ((), ()))

    def project(block):
        wide = jnp.concatenate([full[block, s].reshape(V * YC, XN) for s in range(NA)], axis=1)
        rows = V * YC // 2
        projected = lax.dot_general(wide[:rows], first_half, nt, preferred_element_type=F32)
        projected += lax.dot_general(wide[rows:], second_half, nt, preferred_element_type=F32)
        return wide, projected.astype(BF16).reshape(V // 2, YC, XN)

    def add_gram(block, wide, begin):
        for i in range(2):
            half = (core + 1 + i) % 2
            part = jnp.concatenate(
                [full[block, 2 * half + s].reshape(V * YC, XN) for s in range(2)], axis=1
            )
            term = lax.dot_general(wide, part, tn, preferred_element_type=F32)

            @pl.when(begin)
            def _():
                gacc[i] = term

            @pl.when(jnp.logical_not(begin))
            def _():
                gacc[i] = gacc[i] + term

    def own_layer(block, projected):
        @pl.when(diagonal)
        def _():
            mbuf[:, gy * NC + block] = projected

        @pl.when(jnp.logical_not(diagonal))
        def _():
            pbuf[block] = projected
            project_copy(block, ga).start()

    def gather_gram(c, carry):
        for j in range(1, NA):
            arrived(c, j).wait_recv()
        wide, projected = project(c)
        own_layer(c, projected)
        add_gram(c, wide, c == 0)
        return carry

    lax.fori_loop(0, last, gather_gram, 0)

    @pl.when(first_chip)
    def _():
        def extra(block, carry):
            for j in range(1, NA):
                last_arrived(block, j).wait_recv()
            wide, projected = project(block)

            @pl.when(block == last)
            def _():
                own_layer(block, projected)

            @pl.when(block == NC)
            def _():
                pbuf[block] = projected
                project_copy(block, ga + 2).start()

            add_gram(block, wide, block < 0)
            return carry

        lax.fori_loop(last, NC + 1, extra, 0)

    pair = bring(gacc.at[0], r1, s1_sem, r1_sem, (gy, gz, zhi * 2 + 1 - core))
    pair.start()
    pair.wait_recv()
    g2[...] = (gacc[1] + r1[...]).astype(BF16).reshape(16, 32, 256)

    def plane_copy(j):
        to = (plane + j) % 16
        return bring(g2.at[to], r2.at[plane], s2_sem.at[j], r2_sem.at[plane], plane_device(to))

    def plane_arrived(j):
        source = (plane + j) % 16
        return bring(g2.at[source], r2.at[source], s2_sem.at[j], r2_sem.at[source], plane_device(source))

    def start_plane(j, carry):
        plane_copy(j).start()
        return carry

    for j in range(1, 16):
        start_plane(j, 0)

    def bcast_copy(j):
        peer = (ga + j) % NA
        return bring(ysend, yrecv, bs_sem.at[j], br_sem, (gy, gz, peer))

    @pl.when(diagonal)
    def _():
        def wait_projected(i, carry):
            slot = (gy * NC + i) % 16
            bring(
                pbuf.at[0], mbuf.at[:, slot], ps_sem.at[0], pr_sem.at[slot], ((ga + 1) % NA, gz, ga)
            ).wait_recv()
            return carry

        @pl.when(second_chip)
        def _():
            wait_projected(last, 0)

        lax.fori_loop(NC, 16, wait_projected, 0)
        y_gram = jnp.zeros((256, 256), F32)
        for i in range(V // 2):
            layer = mbuf[i].reshape(256, XN)
            y_gram += lax.dot_general(layer, layer, nt, preferred_element_type=F32)
        product = jnp.dot(
            yft[...], y_gram * (1.0 / 1024.0), precision=lax.Precision.HIGHEST, preferred_element_type=F32
        )
        ysend[...] = product
        yprod_out[...] = product
        for j in (2, 3, 1):
            bcast_copy(j).start()

    def add_plane(j, acc):
        plane_arrived(j).wait_recv()
        return acc + r2[(plane + j) % 16].astype(F32)

    total = g2[plane].astype(F32)
    for j in range(1, 16):
        total = add_plane(j, total)
    s2[...] = total.reshape(4, 8, 256)
    r3[column] = s2[cz]

    def column_copy(j):
        to = (column + j) % 16
        return bring(s2.at[(to // 2) % 4], r3.at[column], s3_sem.at[j], r3_sem.at[column], column_device(to))

    def column_arrived(j):
        source = (column + j) % 16
        return bring(s2.at[0], r3.at[source], s3_sem.at[j], r3_sem.at[source], column_device(source))

    def start_column(j, carry):
        column_copy(j).start()
        return carry

    for j in range(1, 16):
        start_column(j, 0)

    @pl.when(low_y)
    def _():
        y_copy(0).wait_send()

    @pl.when(high_y)
    def _():
        y_copy(1).wait_send()

    @pl.when(low_x)
    def _():
        x_copy(0).wait_send()

    @pl.when(high_x)
    def _():
        x_copy(1).wait_send()

    def sent(c, carry):
        for j in range(1, NA):
            exchange(c, j).wait_send()

        @pl.when(jnp.logical_not(diagonal))
        def _():
            project_copy(c, ga).wait_send()

        return carry

    lax.fori_loop(0, last, sent, 0)

    @pl.when(first_chip)
    def _():
        for m in range(2):
            last_swap(m).wait_send()

        @pl.when(jnp.logical_not(diagonal))
        def _():
            project_copy(last, ga).wait_send()

        project_copy(NC, ga + 2).wait_send()

    @pl.when(second_chip)
    def _():
        for layer in range(NA):
            last_exchange(layer).wait_send()

    pair.wait_send()

    def plane_sent(j, carry):
        plane_copy(j).wait_send()
        return carry

    for j in range(1, 16):
        plane_sent(j, 0)

    @pl.when(diagonal)
    def _():
        for j in range(1, NA):
            bcast_copy(j).wait_send()

    @pl.when(jnp.logical_not(diagonal))
    def _():
        bcast_copy(1).wait_recv()
        yprod_out[...] = yrecv[...]

    def column_wait(j, carry):
        column_arrived(j).wait_recv()
        return carry

    for j in range(1, 16):
        column_wait(j, 0)
    cells = 1.0 / float(V * 256 * 64)
    for half in range(2):
        acc = r3[half]
        for z in range(1, 8):
            acc = acc + r3[2 * z + half]
        gram_out[:, 256 * half : 256 * (half + 1)] = acc * cells

    def column_sent(j, carry):
        column_copy(j).wait_send()
        return carry

    for j in range(1, 16):
        column_sent(j, 0)


def finish(new, gram, product, new_out, gram_out, product_out, sem):
    copies = [
        pltpu.make_async_copy(src, dst, sem.at[i])
        for i, (src, dst) in enumerate(((new, new_out), (gram, gram_out), (product, product_out)))
    ]
    for copy in copies:
        copy.start()
    for copy in copies:
        copy.wait()


def shards(fields, section_start, velocity, diffusivity, reaction, x_factor, y_factor):
    vmem = pl.BlockSpec(memory_space=pltpu.VMEM)
    hbm = pl.BlockSpec(memory_space=pltpu.HBM)
    dma = pltpu.SemaphoreType.DMA
    new_fields, gram, product = pl.pallas_call(
        kernel,
        out_shape=(
            pltpu.VMEM((V, ROWS, XN), F32),
            pltpu.VMEM((8, 512), F32),
            pltpu.VMEM((64, 256), F32),
        ),
        in_specs=[hbm] * 7,
        out_specs=(vmem, vmem, vmem),
        scratch_shapes=[
            pltpu.SMEM((V,), F32),
            pltpu.VMEM((V, V), F32),
            pltpu.VMEM((64, 512), BF16),
            pltpu.VMEM((64, 256), F32),
            pltpu.VMEM((V, PAD + ROWS + PAD, XN), F32),
            pltpu.VMEM((V, ROWS, XN), F32),
            pltpu.VMEM((3, ROWS, XN), F32),
            pltpu.VMEM((2, NC, V, YC, XN), BF16),
            pltpu.VMEM((2, NC, V, YC, XN), BF16),
            pltpu.VMEM((YN, XN), F32),
            pltpu.VMEM((2, YN, XN), F32),
            pltpu.VMEM((YN, XN), F32),
            pltpu.VMEM((NC, ZN, V, YC, XN), BF16),
            pltpu.VMEM((NC + 1, NA, V, YC, XN), BF16),
            pltpu.VMEM((V * YC, 3 * V * YC), BF16),
            pltpu.VMEM((V, YC, XN), F32),
            pltpu.VMEM((2, 512, 256), F32),
            pltpu.VMEM((512, 256), F32),
            pltpu.VMEM((16, 32, 256), BF16),
            pltpu.VMEM((16, 32, 256), BF16),
            pltpu.VMEM((4, 8, 256), F32),
            pltpu.VMEM((16, 8, 256), F32),
            pltpu.VMEM((NC + 1, V // 2, YC, XN), BF16),
            pltpu.VMEM((V // 2, 16, YC, XN), BF16),
            pltpu.VMEM((64, 256), F32),
            pltpu.VMEM((64, 256), F32),
            dma((7,)),
            dma((2, NC)), dma((2, NC)), dma((2,)), dma((2,)), dma((2,)), dma((2,)),
            dma((NC, NA)), dma((NC + 1, NA)),
            dma((NC + 1,)), dma((16,)), dma((NA,)), dma,
            dma, dma, dma((16,)), dma((16,)), dma((16,)), dma((16,)),
        ],
        compiler_params=pltpu.CompilerParams(
            collective_id=0, has_side_effects=True, vmem_limit_bytes=24 << 20
        ),
        name="section",
    )(
        *(
            pltpu.with_memory_space_constraint(array, pltpu.HBM)
            for array in (
                diffusivity,
                reaction,
                x_factor.T,
                y_factor.T,
                fields.reshape(V, ROWS, XN),
                section_start.reshape(V, ROWS, XN),
                velocity.reshape(3, ROWS, XN),
            )
        )
    )
    new_fields, gram, product = pl.pallas_call(
        finish,
        out_shape=(
            jax.ShapeDtypeStruct((V, ROWS, XN), F32),
            jax.ShapeDtypeStruct((8, 512), F32),
            jax.ShapeDtypeStruct((64, 256), F32),
        ),
        in_specs=[pl.BlockSpec(memory_space=pl.ANY)] * 3,
        out_specs=(hbm,) * 3,
        scratch_shapes=[dma((3,))],
        name="finish", compiler_params=pltpu.CompilerParams(vmem_limit_bytes=1 << 20),
    )(new_fields, gram, product)
    return new_fields.reshape(V, YN, ZN, XN), gram, product.T[None]


def solution(mesh):
    in_specs = (
        P(None, "gy", "gz", "ga"),
        P(None, "gy", "gz", "ga"),
        P(None, "gy", "gz", "ga"),
        P(),
        P(),
        P(),
        P(),
    )
    out_specs = (P(None, "gy", "gz", "ga"), P(("gy", "gz"), None), P(("gz", "gy"), None, None))
    return jax.shard_map(shards, mesh=mesh, in_specs=in_specs, out_specs=out_specs, check_vma=False)
```

```python
import functools

import jax
import jax.numpy as jnp
from jax import lax
from jax.experimental import pallas as pl
from jax.experimental.pallas import tpu as pltpu
from jax.sharding import PartitionSpec as P

time_step = 0.4

MESH = pl.DeviceIdType.MESH
V = 16
YN = 64
ZN = 4
XN = 128
ROWS = YN * ZN
NC = 4
YC = YN // NC
CR = YC * ZN
PAD = 8
NY, NZ, NA = 4, 16, 4
F32, BF16 = jnp.float32, jnp.bfloat16


def bring(src, dst, send_sem, recv_sem, device):
    return pltpu.make_async_remote_copy(
        src_ref=src, dst_ref=dst, send_sem=send_sem, recv_sem=recv_sem, device_id=device, device_id_type=MESH
    )


def kernel(
    dif_in, rea_in, xft_in, yft_in, fields, start, vel,
    new_out, gram_out, yprod_out,
    dif, rea, xft, yft, fbuf, sbuf, vbuf, zsend, zrecv, xpack, xrecv, xcomb, snap, full, kmat, rfb,
    gacc, r1, g2, r2, s2, r3, pbuf, mbuf, ysend, yrecv,
    load_sem, zs_sem, zr_sem, ys_sem, yr_sem, xs_sem, xr_sem, as_sem, ar_sem,
    ps_sem, pr_sem, bs_sem, br_sem, s1_sem, r1_sem, s2_sem, r2_sem, s3_sem, r3_sem,
):
    gy, gz, ga = lax.axis_index("gy"), lax.axis_index("gz"), lax.axis_index("ga")
    cy, cz = gz // 4, gz % 4
    zhi, core = ga // 2, ga % 2
    plane = gy * 4 + cy
    column = (zhi * 4 + cz) * 2 + core
    buffer_slab = ga == NA - 1
    diagonal = gy == ga
    at_end = jnp.logical_or(cz == 0, cz == 3)
    plain = jnp.logical_not(at_end)
    first_chip = jnp.logical_and(at_end, zhi == 0)
    second_chip = jnp.logical_and(at_end, zhi == 1)
    to_second = jnp.logical_and(first_chip, gy != ga + 2)
    from_first = jnp.logical_and(second_chip, diagonal)
    inner_slab = ga < NA - 1

    def plane_device(index):
        return (index // 4, (index % 4) * 4 + cz, ga)

    def column_device(index):
        return (gy, cy * 4 + (index // 2) % 4, (index // 8) * 2 + index % 2)

    load_f = pltpu.make_async_copy(fields, fbuf.at[:, pl.ds(PAD, ROWS), :], load_sem.at[0])
    load_s = pltpu.make_async_copy(start, sbuf, load_sem.at[1])
    load_v = pltpu.make_async_copy(vel, vbuf, load_sem.at[2])
    load_small = [
        pltpu.make_async_copy(src, dst, load_sem.at[3 + i])
        for i, (src, dst) in enumerate(((rea_in, rea), (dif_in, dif), (xft_in, xft), (yft_in, yft)))
    ]
    load_f.start()
    load_small[0].start()
    load_s.start()
    load_v.start()
    for copy in load_small[1:]:
        copy.start()

    barrier = pltpu.get_barrier_semaphore()
    wrap_up = jnp.logical_and(cz == 3, gz < NZ - 1)
    wrap_down = jnp.logical_and(cz == 0, gz > 0)

    @pl.when(wrap_up)
    def _():
        pl.semaphore_signal(barrier, inc=1, device_id=(gy, gz + 1, ga), device_id_type=MESH)

    @pl.when(wrap_down)
    def _():
        pl.semaphore_signal(barrier, inc=1, device_id=(gy, gz - 1, ga), device_id_type=MESH)

    def greet(j, carry):
        pl.semaphore_signal(barrier, inc=1, device_id=plane_device((plane + j) % 16), device_id_type=MESH)
        pl.semaphore_signal(barrier, inc=1, device_id=column_device((column + j) % 16), device_id_type=MESH)
        return carry

    for j in range(1, 16):
        greet(j, 0)

    @pl.when(to_second)
    def _():
        pl.semaphore_signal(barrier, inc=1, device_id=(ga + 2, gz, ga + 2), device_id_type=MESH)

    @pl.when(from_first)
    def _():
        for j in range(1, NY):
            pl.semaphore_signal(barrier, inc=1, device_id=((gy + j) % NY, gz, ga - 2), device_id_type=MESH)

    @pl.when(gy == 0)
    def _():
        fbuf[:, 0:PAD, :] = jnp.zeros((V, PAD, XN), F32)

    @pl.when(gy == NY - 1)
    def _():
        fbuf[:, PAD + ROWS : PAD + ROWS + PAD, :] = jnp.zeros((V, PAD, XN), F32)

    @pl.when(gz == 0)
    def _():
        zrecv[0] = jnp.zeros((NC, V, YC, XN), BF16)

    @pl.when(gz == NZ - 1)
    def _():
        zrecv[1] = jnp.zeros((NC, V, YC, XN), BF16)

    @pl.when(ga == 0)
    def _():
        xrecv[0] = jnp.zeros((YN, XN), F32)

    load_f.wait()

    @pl.when(inner_slab)
    def _():
        def face(v, carry):
            for side, z in ((0, 0), (1, ZN - 1)):
                for c in range(NC):
                    piece = fbuf[v, pl.ds(PAD + c * CR + z, YC, stride=ZN), :]
                    zsend[side, c, v] = piece.astype(BF16)
            return carry

        lax.fori_loop(0, V, face, 0)

    pl.semaphore_wait(
        barrier,
        30 + wrap_up.astype(jnp.int32) + wrap_down.astype(jnp.int32)
        + to_second.astype(jnp.int32) + 3 * from_first.astype(jnp.int32),
    )

    def z_copy(side, c):
        return bring(
            zsend.at[side, c], zrecv.at[1 - side, c], zs_sem.at[side, c], zr_sem.at[1 - side, c],
            (gy, gz - 1 + 2 * side, ga),
        )

    low_z = jnp.logical_and(inner_slab, gz > 0)
    high_z = jnp.logical_and(inner_slab, gz < NZ - 1)
    low_y = jnp.logical_and(inner_slab, gy > 0)
    high_y = jnp.logical_and(inner_slab, gy < NY - 1)

    def y_copy(side):
        src = fields.at[:, pl.ds((ROWS - PAD) * side, PAD), :]
        dst = fbuf.at[:, pl.ds((PAD + ROWS) * (1 - side), PAD), :]
        return bring(src, dst, ys_sem.at[side], yr_sem.at[1 - side], (gy - 1 + 2 * side, gz, ga))

    def start_faces(c):
        @pl.when(low_z)
        def _():
            z_copy(0, c).start()

        @pl.when(high_z)
        def _():
            z_copy(1, c).start()

    def faces_sent(c):
        @pl.when(low_z)
        def _():
            z_copy(0, c).wait_send()

        @pl.when(high_z)
        def _():
            z_copy(1, c).wait_send()

    start_faces(0)

    @pl.when(low_y)
    def _():
        y_copy(0).start()

    @pl.when(high_y)
    def _():
        y_copy(1).start()

    lane = lax.broadcasted_iota(jnp.int32, (YN, XN), 1)

    def pack(v, acc):
        for z in range(ZN):
            at = 2 * (v * ZN + z)
            piece = fbuf[v, pl.ds(PAD + z, YN, stride=ZN), :]
            moved = pltpu.roll(piece, at + 1, 1)
            acc = jnp.where(jnp.logical_or(lane == at, lane == at + 1), moved, acc)
        return acc

    xpack[...] = lax.fori_loop(0, V, pack, jnp.zeros((YN, XN), F32))

    def x_copy(side):
        return bring(
            xpack, xrecv.at[1 - side], xs_sem.at[side], xr_sem.at[1 - side], (gy, gz, ga - 1 + 2 * side)
        )

    low_x = ga > 0
    high_x = ga < NA - 2

    @pl.when(low_x)
    def _():
        x_copy(0).start()

    @pl.when(high_x)
    def _():
        x_copy(1).start()

    for c in range(1, NC):
        start_faces(c)

    def exchange(c, j):
        peer = (ga + j) % NA
        return bring(snap.at[c, peer], full.at[c, ga], as_sem.at[c, j], ar_sem.at[c, ga], (gy, gz, peer))

    def arrived(c, j):
        slab = (ga + j) % NA
        return bring(snap.at[c, slab], full.at[c, slab], as_sem.at[c, j], ar_sem.at[c, slab], (gy, gz, slab))

    last = NC - 1

    def last_exchange(layer):
        return bring(
            snap.at[last, layer], full.at[last + layer // 2, ga], as_sem.at[last, layer],
            ar_sem.at[last + layer // 2, ga], (gy, gz, layer % 2),
        )

    def last_swap(m):
        return bring(
            snap.at[last, 2 * m + 1 - core], full.at[last + m, ga], as_sem.at[last, m],
            ar_sem.at[last + m, ga], (gy, gz, 1 - core),
        )

    def last_arrived(block, j):
        slab = (ga + j) % NA
        return bring(
            snap.at[0, slab], full.at[block, slab], as_sem.at[0, j], ar_sem.at[block, slab], (gy, gz, slab)
        )

    def hand_over(c):
        @pl.when(jnp.logical_or(plain, c < last))
        def _():
            full[c, ga] = snap[c, ga]
            for j in (2, 3, 1):
                exchange(c, j).start()

        @pl.when(jnp.logical_and(c == last, first_chip))
        def _():
            for m in range(2):
                last_swap(m).start()
            for m in range(2):
                full[last + m, ga] = snap[last, 2 * m + core]

        @pl.when(jnp.logical_and(c == last, second_chip))
        def _():
            for layer in range(NA):
                last_exchange(layer).start()

    load_small[0].wait()

    low16 = lax.broadcasted_iota(jnp.int32, (V * YC, V), 0) // YC
    spread = (low16 == lax.broadcasted_iota(jnp.int32, (V * YC, V), 1)).astype(F32).astype(BF16)
    rows_at = lax.broadcasted_iota(jnp.int32, (V * YC, V * YC), 0) % YC
    cols_at = lax.broadcasted_iota(jnp.int32, (V * YC, V * YC), 1) % YC
    same = rows_at == cols_at
    rate = (0.25 * time_step) * rea[...]
    rate_high = rate.astype(BF16)
    rate_low = (rate - rate_high.astype(F32)).astype(BF16)
    for part, piece in enumerate((rate_high, rate_high, rate_low)):
        tall = jnp.dot(spread, piece, preferred_element_type=F32).astype(BF16)
        square = lax.dot_general(tall, spread, (((1,), (1,)), ((), ())), preferred_element_type=F32)
        kmat[:, V * YC * part : V * YC * (part + 1)] = jnp.where(same, square, 0.0).astype(BF16)

    load_s.wait()
    load_v.wait()
    for copy in load_small[1:]:
        copy.wait()

    @pl.when(buffer_slab)
    def _():
        def chunk(c, carry):
            def variable(v, inner):
                new_out[v, pl.ds(c * CR, CR), :] = fbuf[v, pl.ds(PAD + c * CR, CR), :]
                for z in range(ZN):
                    piece = fbuf[v, pl.ds(PAD + c * CR + z, YC, stride=ZN), :]
                    snap[c, z, v] = piece.astype(BF16)
                return inner

            lax.fori_loop(0, V, variable, 0)
            hand_over(c)
            return carry

        lax.fori_loop(0, NC, chunk, 0)

    @pl.when(inner_slab)
    def _():
        @pl.when(gy > 0)
        def _():
            y_copy(1).wait_recv()

        @pl.when(gy < NY - 1)
        def _():
            y_copy(0).wait_recv()

        @pl.when(ga > 0)
        def _():
            x_copy(1).wait_recv()

        x_copy(0).wait_recv()
        xcomb[...] = jnp.where(lane % 2 == 0, xrecv[0], xrecv[1])
        edge = lax.broadcasted_iota(jnp.int32, (YC, XN), 1)

        def chunk(c, carry):
            @pl.when(gz > 0)
            def _():
                z_copy(1, c).wait_recv()

            @pl.when(gz < NZ - 1)
            def _():
                z_copy(0, c).wait_recv()

            faces_sent(c)

            for z in range(ZN):
                first = PAD + c * CR + z
                stack = jnp.concatenate(
                    [fbuf[v, pl.ds(first, YC, stride=ZN), :] for v in range(V)], axis=0
                )
                high = stack.astype(BF16)
                low = (stack - high.astype(F32)).astype(BF16)
                reacted = jnp.dot(
                    kmat[...], jnp.concatenate([high, low, high], axis=0), preferred_element_type=F32
                )
                rfb[...] = reacted.reshape(V, YC, XN)
                scale = 0.125 * time_step
                vx, vy, vz = (scale * vbuf[d, pl.ds(c * CR + z, YC, stride=ZN), :] for d in range(3))
                faces = xcomb[pl.ds(c * YC, YC), :]

                def variable(v, inner):
                    here = fbuf[v, pl.ds(first, YC, stride=ZN), :]
                    y_plus = fbuf[v, pl.ds(first + ZN, YC, stride=ZN), :]
                    y_minus = fbuf[v, pl.ds(first - ZN, YC, stride=ZN), :]
                    if z < ZN - 1:
                        z_plus = fbuf[v, pl.ds(first + 1, YC, stride=ZN), :]
                    else:
                        z_plus = zrecv[1, c, v].astype(F32)
                    if z > 0:
                        z_minus = fbuf[v, pl.ds(first - 1, YC, stride=ZN), :]
                    else:
                        z_minus = zrecv[0, c, v].astype(F32)
                    at = 2 * (v * ZN + z)
                    moved = pltpu.roll(faces, XN - 1 - at, 1)
                    x_plus = pltpu.roll(jnp.where(edge == 0, moved, here), XN - 1, 1)
                    x_minus = pltpu.roll(jnp.where(edge == XN - 1, moved, here), 1, 1)
                    laplace = (
                        (x_plus + x_minus) + (y_plus + y_minus) + (z_plus + z_minus) - 6.0 * here
                    )
                    advection = (
                        vx * (x_plus - x_minus) + vy * (y_plus - y_minus) + vz * (z_plus - z_minus)
                    )
                    began = sbuf[v, pl.ds(c * CR + z, YC, stride=ZN), :]
                    value = (
                        0.75 * began + 0.25 * here
                        + ((0.25 * time_step) * dif[v]) * laplace - advection + rfb[v]
                    )
                    new_out[v, pl.ds(c * CR + z, YC, stride=ZN), :] = value
                    snap[c, z, v] = value.astype(BF16)
                    return inner

                lax.fori_loop(0, V, variable, 0, unroll=True)
            hand_over(c)
            return carry

        lax.fori_loop(0, NC, chunk, 0)

    def project_copy(block, layer):
        slot = gy * NC + jnp.minimum(block, last)
        return bring(pbuf.at[block], mbuf.at[:, slot], ps_sem.at[block], pr_sem.at[slot], (layer, gz, layer))

    zero = jnp.zeros_like(xft[...])
    first_half = jnp.concatenate([xft[...], zero], axis=0)
    second_half = jnp.concatenate([zero, xft[...]], axis=0)
    nt = (((1,), (1,)), ((), ()))
    tn = (((0,), (0,)), ((), ()))

    def project(block):
        wide = jnp.concatenate([full[block, s].reshape(V * YC, XN) for s in range(NA)], axis=1)
        rows = V * YC // 2
        projected = lax.dot_general(wide[:rows], first_half, nt, preferred_element_type=F32)
        projected += lax.dot_general(wide[rows:], second_half, nt, preferred_element_type=F32)
        return wide, projected.astype(BF16).reshape(V // 2, YC, XN)

    def add_gram(block, wide, begin):
        for i in range(2):
            half = (core + 1 + i) % 2
            part = jnp.concatenate(
                [full[block, 2 * half + s].reshape(V * YC, XN) for s in range(2)], axis=1
            )
            term = lax.dot_general(wide, part, tn, preferred_element_type=F32)

            @pl.when(begin)
            def _():
                gacc[i] = term

            @pl.when(jnp.logical_not(begin))
            def _():
                gacc[i] = gacc[i] + term

    def own_layer(block, projected):
        @pl.when(diagonal)
        def _():
            mbuf[:, gy * NC + block] = projected

        @pl.when(jnp.logical_not(diagonal))
        def _():
            pbuf[block] = projected
            project_copy(block, ga).start()

    def gather_gram(c, carry):
        for j in range(1, NA):
            arrived(c, j).wait_recv()
        wide, projected = project(c)
        own_layer(c, projected)
        add_gram(c, wide, c == 0)
        return carry

    lax.fori_loop(0, last, gather_gram, 0)

    @pl.when(plain)
    def _():
        gather_gram(jnp.int32(last), 0)

    @pl.when(first_chip)
    def _():
        def extra(block, carry):
            for j in range(1, NA):
                last_arrived(block, j).wait_recv()
            wide, projected = project(block)

            @pl.when(block == last)
            def _():
                own_layer(block, projected)

            @pl.when(block == NC)
            def _():
                pbuf[block] = projected
                project_copy(block, ga + 2).start()

            add_gram(block, wide, block < 0)
            return carry

        lax.fori_loop(last, NC + 1, extra, 0)

    pair = bring(gacc.at[0], r1, s1_sem, r1_sem, (gy, gz, zhi * 2 + 1 - core))
    pair.start()
    pair.wait_recv()
    g2[...] = (gacc[1] + r1[...]).astype(BF16).reshape(16, 32, 256)

    def plane_copy(j):
        to = (plane + j) % 16
        return bring(g2.at[to], r2.at[plane], s2_sem.at[j], r2_sem.at[plane], plane_device(to))

    def plane_arrived(j):
        source = (plane + j) % 16
        return bring(g2.at[source], r2.at[source], s2_sem.at[j], r2_sem.at[source], plane_device(source))

    def start_plane(j, carry):
        plane_copy(j).start()
        return carry

    for j in range(1, 16):
        start_plane(j, 0)

    def bcast_copy(j):
        peer = (ga + j) % NA
        return bring(ysend, yrecv, bs_sem.at[j], br_sem, (gy, gz, peer))

    @pl.when(diagonal)
    def _():
        def wait_projected(i, carry):
            slot = (gy * NC + i) % 16
            bring(
                pbuf.at[0], mbuf.at[:, slot], ps_sem.at[0], pr_sem.at[slot], ((ga + 1) % NA, gz, ga)
            ).wait_recv()
            return carry

        @pl.when(second_chip)
        def _():
            wait_projected(last, 0)

        lax.fori_loop(NC, 16, wait_projected, 0)
        y_gram = jnp.zeros((256, 256), F32)
        for i in range(V // 2):
            layer = mbuf[i].reshape(256, XN)
            y_gram += lax.dot_general(layer, layer, nt, preferred_element_type=F32)
        product = jnp.dot(
            yft[...], y_gram * (1.0 / 1024.0), precision=lax.Precision.HIGHEST, preferred_element_type=F32
        )
        ysend[...] = product
        yprod_out[...] = product
        for j in (2, 3, 1):
            bcast_copy(j).start()

    def add_plane(j, acc):
        plane_arrived(j).wait_recv()
        return acc + r2[(plane + j) % 16].astype(F32)

    total = g2[plane].astype(F32)
    for j in range(1, 16):
        total = add_plane(j, total)
    s2[...] = total.reshape(4, 8, 256)
    r3[column] = s2[cz]

    def column_copy(j):
        to = (column + j) % 16
        return bring(s2.at[(to // 2) % 4], r3.at[column], s3_sem.at[j], r3_sem.at[column], column_device(to))

    def column_arrived(j):
        source = (column + j) % 16
        return bring(s2.at[0], r3.at[source], s3_sem.at[j], r3_sem.at[source], column_device(source))

    def start_column(j, carry):
        column_copy(j).start()
        return carry

    for j in range(1, 16):
        start_column(j, 0)

    @pl.when(low_y)
    def _():
        y_copy(0).wait_send()

    @pl.when(high_y)
    def _():
        y_copy(1).wait_send()

    @pl.when(low_x)
    def _():
        x_copy(0).wait_send()

    @pl.when(high_x)
    def _():
        x_copy(1).wait_send()

    def sent(c, carry):
        for j in range(1, NA):
            exchange(c, j).wait_send()

        @pl.when(jnp.logical_not(diagonal))
        def _():
            project_copy(c, ga).wait_send()

        return carry

    lax.fori_loop(0, last, sent, 0)

    @pl.when(plain)
    def _():
        sent(last, 0)

    @pl.when(first_chip)
    def _():
        for m in range(2):
            last_swap(m).wait_send()

        @pl.when(jnp.logical_not(diagonal))
        def _():
            project_copy(last, ga).wait_send()

        project_copy(NC, ga + 2).wait_send()

    @pl.when(second_chip)
    def _():
        for layer in range(NA):
            last_exchange(layer).wait_send()

    pair.wait_send()

    def plane_sent(j, carry):
        plane_copy(j).wait_send()
        return carry

    for j in range(1, 16):
        plane_sent(j, 0)

    @pl.when(diagonal)
    def _():
        for j in range(1, NA):
            bcast_copy(j).wait_send()

    @pl.when(jnp.logical_not(diagonal))
    def _():
        bcast_copy(1).wait_recv()
        yprod_out[...] = yrecv[...]

    def column_wait(j, carry):
        column_arrived(j).wait_recv()
        return carry

    for j in range(1, 16):
        column_wait(j, 0)
    cells = 1.0 / float(V * 256 * 64)
    for half in range(2):
        acc = r3[half]
        for z in range(1, 8):
            acc = acc + r3[2 * z + half]
        gram_out[:, 256 * half : 256 * (half + 1)] = acc * cells

    def column_sent(j, carry):
        column_copy(j).wait_send()
        return carry

    for j in range(1, 16):
        column_sent(j, 0)


def finish(new, gram, product, new_out, gram_out, product_out, sem):
    copies = [
        pltpu.make_async_copy(src, dst, sem.at[i])
        for i, (src, dst) in enumerate(((new, new_out), (gram, gram_out), (product, product_out)))
    ]
    for copy in copies:
        copy.start()
    for copy in copies:
        copy.wait()


def shards(fields, section_start, velocity, diffusivity, reaction, x_factor, y_factor):
    vmem = pl.BlockSpec(memory_space=pltpu.VMEM)
    hbm = pl.BlockSpec(memory_space=pltpu.HBM)
    dma = pltpu.SemaphoreType.DMA
    new_fields, gram, product = pl.pallas_call(
        kernel,
        out_shape=(
            pltpu.VMEM((V, ROWS, XN), F32),
            pltpu.VMEM((8, 512), F32),
            pltpu.VMEM((64, 256), F32),
        ),
        in_specs=[hbm] * 7,
        out_specs=(vmem, vmem, vmem),
        scratch_shapes=[
            pltpu.SMEM((V,), F32),
            pltpu.VMEM((V, V), F32),
            pltpu.VMEM((64, 512), BF16),
            pltpu.VMEM((64, 256), F32),
            pltpu.VMEM((V, PAD + ROWS + PAD, XN), F32),
            pltpu.VMEM((V, ROWS, XN), F32),
            pltpu.VMEM((3, ROWS, XN), F32),
            pltpu.VMEM((2, NC, V, YC, XN), BF16),
            pltpu.VMEM((2, NC, V, YC, XN), BF16),
            pltpu.VMEM((YN, XN), F32),
            pltpu.VMEM((2, YN, XN), F32),
            pltpu.VMEM((YN, XN), F32),
            pltpu.VMEM((NC, ZN, V, YC, XN), BF16),
            pltpu.VMEM((NC + 1, NA, V, YC, XN), BF16),
            pltpu.VMEM((V * YC, 3 * V * YC), BF16),
            pltpu.VMEM((V, YC, XN), F32),
            pltpu.VMEM((2, 512, 256), F32),
            pltpu.VMEM((512, 256), F32),
            pltpu.VMEM((16, 32, 256), BF16),
            pltpu.VMEM((16, 32, 256), BF16),
            pltpu.VMEM((4, 8, 256), F32),
            pltpu.VMEM((16, 8, 256), F32),
            pltpu.VMEM((NC + 1, V // 2, YC, XN), BF16),
            pltpu.VMEM((V // 2, 16, YC, XN), BF16),
            pltpu.VMEM((64, 256), F32),
            pltpu.VMEM((64, 256), F32),
            dma((7,)),
            dma((2, NC)), dma((2, NC)), dma((2,)), dma((2,)), dma((2,)), dma((2,)),
            dma((NC, NA)), dma((NC + 1, NA)),
            dma((NC + 1,)), dma((16,)), dma((NA,)), dma,
            dma, dma, dma((16,)), dma((16,)), dma((16,)), dma((16,)),
        ],
        compiler_params=pltpu.CompilerParams(
            collective_id=0, has_side_effects=True, vmem_limit_bytes=24 << 20
        ),
        name="section",
    )(
        *(
            pltpu.with_memory_space_constraint(array, pltpu.HBM)
            for array in (
                diffusivity,
                reaction,
                x_factor.T,
                y_factor.T,
                fields.reshape(V, ROWS, XN),
                section_start.reshape(V, ROWS, XN),
                velocity.reshape(3, ROWS, XN),
            )
        )
    )
    new_fields, gram, product = pl.pallas_call(
        finish,
        out_shape=(
            jax.ShapeDtypeStruct((V, ROWS, XN), F32),
            jax.ShapeDtypeStruct((8, 512), F32),
            jax.ShapeDtypeStruct((64, 256), F32),
        ),
        in_specs=[pl.BlockSpec(memory_space=pl.ANY)] * 3,
        out_specs=(hbm,) * 3,
        scratch_shapes=[dma((3,))],
        name="finish", compiler_params=pltpu.CompilerParams(vmem_limit_bytes=1 << 20),
    )(new_fields, gram, product)
    return new_fields.reshape(V, YN, ZN, XN), gram, product.T[None]


def solution(mesh):
    in_specs = (
        P(None, "gy", "gz", "ga"),
        P(None, "gy", "gz", "ga"),
        P(None, "gy", "gz", "ga"),
        P(),
        P(),
        P(),
        P(),
    )
    out_specs = (P(None, "gy", "gz", "ga"), P(("gy", "gz"), None), P(("gz", "gy"), None, None))
    return jax.shard_map(shards, mesh=mesh, in_specs=in_specs, out_specs=out_specs, check_vma=False)
```

```python
import functools

import jax
import jax.numpy as jnp
from jax import lax
from jax.experimental import pallas as pl
from jax.experimental.pallas import tpu as pltpu
from jax.sharding import PartitionSpec as P

time_step = 0.4

MESH = pl.DeviceIdType.MESH
V = 16
YN = 64
ZN = 4
XN = 128
ROWS = YN * ZN
NC = 4
YC = YN // NC
CR = YC * ZN
PAD = 8
NY, NZ, NA = 4, 16, 4
F32, BF16 = jnp.float32, jnp.bfloat16


def bring(src, dst, send_sem, recv_sem, device):
    return pltpu.make_async_remote_copy(
        src_ref=src, dst_ref=dst, send_sem=send_sem, recv_sem=recv_sem, device_id=device, device_id_type=MESH
    )


def kernel(
    dif_in, rea_in, xft_in, yft_in, fields, start, vel,
    new_out, gram_out, yprod_out,
    dif, rea, xft, yft, fbuf, sbuf, vbuf, zsend, zrecv, xpack, xrecv, xcomb, snap, full, kmat, rfb,
    gacc, r1, g2, r2, s2, r3, pbuf, mbuf, ysend, yrecv,
    load_sem, zs_sem, zr_sem, ys_sem, yr_sem, xs_sem, xr_sem, as_sem, ar_sem,
    ps_sem, pr_sem, bs_sem, br_sem, s1_sem, r1_sem, s2_sem, r2_sem, s3_sem, r3_sem,
):
    gy, gz, ga = lax.axis_index("gy"), lax.axis_index("gz"), lax.axis_index("ga")
    cy, cz = gz // 4, gz % 4
    zhi, core = ga // 2, ga % 2
    plane = gy * 4 + cy
    column = (zhi * 4 + cz) * 2 + core
    buffer_slab = ga == NA - 1
    diagonal = gy == ga
    at_end = jnp.logical_or(cz == 0, cz == 3)
    plain = jnp.logical_not(at_end)
    first_chip = jnp.logical_and(at_end, zhi == 0)
    second_chip = jnp.logical_and(at_end, zhi == 1)
    to_second = jnp.logical_and(first_chip, gy != ga + 2)
    from_first = jnp.logical_and(second_chip, diagonal)
    inner_slab = ga < NA - 1

    def plane_device(index):
        return (index // 4, (index % 4) * 4 + cz, ga)

    def column_device(index):
        return (gy, cy * 4 + (index // 2) % 4, (index // 8) * 2 + index % 2)

    load_f = pltpu.make_async_copy(fields, fbuf.at[:, pl.ds(PAD, ROWS), :], load_sem.at[0])
    load_s = pltpu.make_async_copy(start, sbuf, load_sem.at[1])
    load_v = pltpu.make_async_copy(vel, vbuf, load_sem.at[2])
    load_small = [
        pltpu.make_async_copy(src, dst, load_sem.at[3 + i])
        for i, (src, dst) in enumerate(((rea_in, rea), (dif_in, dif), (xft_in, xft), (yft_in, yft)))
    ]
    load_f.start()
    load_small[0].start()
    load_s.start()
    load_v.start()
    for copy in load_small[1:]:
        copy.start()

    barrier = pltpu.get_barrier_semaphore()
    wrap_up = jnp.logical_and(cz == 3, gz < NZ - 1)
    wrap_down = jnp.logical_and(cz == 0, gz > 0)

    @pl.when(wrap_up)
    def _():
        pl.semaphore_signal(barrier, inc=1, device_id=(gy, gz + 1, ga), device_id_type=MESH)

    @pl.when(wrap_down)
    def _():
        pl.semaphore_signal(barrier, inc=1, device_id=(gy, gz - 1, ga), device_id_type=MESH)

    def greet(j, carry):
        pl.semaphore_signal(barrier, inc=1, device_id=plane_device((plane + j) % 16), device_id_type=MESH)
        pl.semaphore_signal(barrier, inc=1, device_id=column_device((column + j) % 16), device_id_type=MESH)
        return carry

    for j in range(1, 16):
        greet(j, 0)

    @pl.when(to_second)
    def _():
        pl.semaphore_signal(barrier, inc=1, device_id=(ga + 2, gz, ga + 2), device_id_type=MESH)

    @pl.when(from_first)
    def _():
        for j in range(1, NY):
            pl.semaphore_signal(barrier, inc=1, device_id=((gy + j) % NY, gz, ga - 2), device_id_type=MESH)

    @pl.when(gy == 0)
    def _():
        fbuf[:, 0:PAD, :] = jnp.zeros((V, PAD, XN), F32)

    @pl.when(gy == NY - 1)
    def _():
        fbuf[:, PAD + ROWS : PAD + ROWS + PAD, :] = jnp.zeros((V, PAD, XN), F32)

    @pl.when(gz == 0)
    def _():
        zrecv[0] = jnp.zeros((NC, V, YC, XN), BF16)

    @pl.when(gz == NZ - 1)
    def _():
        zrecv[1] = jnp.zeros((NC, V, YC, XN), BF16)

    @pl.when(ga == 0)
    def _():
        xrecv[0] = jnp.zeros((YN, XN), F32)

    load_f.wait()

    @pl.when(inner_slab)
    def _():
        def face(v, carry):
            for side, z in ((0, 0), (1, ZN - 1)):
                for c in range(NC):
                    piece = fbuf[v, pl.ds(PAD + c * CR + z, YC, stride=ZN), :]
                    zsend[side, c, v] = piece.astype(BF16)
            return carry

        lax.fori_loop(0, V, face, 0)

    pl.semaphore_wait(
        barrier,
        30 + wrap_up.astype(jnp.int32) + wrap_down.astype(jnp.int32)
        + to_second.astype(jnp.int32) + 3 * from_first.astype(jnp.int32),
    )

    def z_copy(side, c):
        return bring(
            zsend.at[side, c], zrecv.at[1 - side, c], zs_sem.at[side, c], zr_sem.at[1 - side, c],
            (gy, gz - 1 + 2 * side, ga),
        )

    low_z = jnp.logical_and(inner_slab, gz > 0)
    high_z = jnp.logical_and(inner_slab, gz < NZ - 1)
    low_y = jnp.logical_and(inner_slab, gy > 0)
    high_y = jnp.logical_and(inner_slab, gy < NY - 1)

    def y_copy(side):
        src = fields.at[:, pl.ds((ROWS - PAD) * side, PAD), :]
        dst = fbuf.at[:, pl.ds((PAD + ROWS) * (1 - side), PAD), :]
        return bring(src, dst, ys_sem.at[side], yr_sem.at[1 - side], (gy - 1 + 2 * side, gz, ga))

    def start_faces(c):
        @pl.when(low_z)
        def _():
            z_copy(0, c).start()

        @pl.when(high_z)
        def _():
            z_copy(1, c).start()

    def faces_sent(c):
        @pl.when(low_z)
        def _():
            z_copy(0, c).wait_send()

        @pl.when(high_z)
        def _():
            z_copy(1, c).wait_send()

    start_faces(0)

    @pl.when(low_y)
    def _():
        y_copy(0).start()

    @pl.when(high_y)
    def _():
        y_copy(1).start()

    lane = lax.broadcasted_iota(jnp.int32, (YN, XN), 1)

    def pack(v, acc):
        for z in range(ZN):
            at = 2 * (v * ZN + z)
            piece = fbuf[v, pl.ds(PAD + z, YN, stride=ZN), :]
            moved = pltpu.roll(piece, at + 1, 1)
            acc = jnp.where(jnp.logical_or(lane == at, lane == at + 1), moved, acc)
        return acc

    xpack[...] = lax.fori_loop(0, V, pack, jnp.zeros((YN, XN), F32))

    def x_copy(side):
        return bring(
            xpack, xrecv.at[1 - side], xs_sem.at[side], xr_sem.at[1 - side], (gy, gz, ga - 1 + 2 * side)
        )

    low_x = ga > 0
    high_x = ga < NA - 2

    @pl.when(low_x)
    def _():
        x_copy(0).start()

    @pl.when(high_x)
    def _():
        x_copy(1).start()

    start_faces(1)
    start_faces(2)

    def exchange(c, j):
        peer = (ga + j) % NA
        return bring(snap.at[c, peer], full.at[c, ga], as_sem.at[c, j], ar_sem.at[c, ga], (gy, gz, peer))

    def arrived(c, j):
        slab = (ga + j) % NA
        return bring(snap.at[c, slab], full.at[c, slab], as_sem.at[c, j], ar_sem.at[c, slab], (gy, gz, slab))

    last = NC - 1

    def last_exchange(layer):
        return bring(
            snap.at[last, layer], full.at[last + layer // 2, ga], as_sem.at[last, layer],
            ar_sem.at[last + layer // 2, ga], (gy, gz, layer % 2),
        )

    def last_swap(m):
        return bring(
            snap.at[last, 2 * m + 1 - core], full.at[last + m, ga], as_sem.at[last, m],
            ar_sem.at[last + m, ga], (gy, gz, 1 - core),
        )

    def last_arrived(block, j):
        slab = (ga + j) % NA
        return bring(
            snap.at[0, slab], full.at[block, slab], as_sem.at[0, j], ar_sem.at[block, slab], (gy, gz, slab)
        )

    def hand_over(c):
        @pl.when(jnp.logical_or(plain, c < last))
        def _():
            full[c, ga] = snap[c, ga]
            for j in (2, 3, 1):
                exchange(c, j).start()

        @pl.when(jnp.logical_and(c == last, first_chip))
        def _():
            for m in range(2):
                last_swap(m).start()
            for m in range(2):
                full[last + m, ga] = snap[last, 2 * m + core]

        @pl.when(jnp.logical_and(c == last, second_chip))
        def _():
            for layer in range(NA):
                last_exchange(layer).start()

    load_small[0].wait()

    low16 = lax.broadcasted_iota(jnp.int32, (V * YC, V), 0) // YC
    spread = (low16 == lax.broadcasted_iota(jnp.int32, (V * YC, V), 1)).astype(F32).astype(BF16)
    rows_at = lax.broadcasted_iota(jnp.int32, (V * YC, V * YC), 0) % YC
    cols_at = lax.broadcasted_iota(jnp.int32, (V * YC, V * YC), 1) % YC
    same = rows_at == cols_at
    rate = (0.25 * time_step) * rea[...]
    rate_high = rate.astype(BF16)
    rate_low = (rate - rate_high.astype(F32)).astype(BF16)
    for part, piece in enumerate((rate_high, rate_high, rate_low)):
        tall = jnp.dot(spread, piece, preferred_element_type=F32).astype(BF16)
        square = lax.dot_general(tall, spread, (((1,), (1,)), ((), ())), preferred_element_type=F32)
        kmat[:, V * YC * part : V * YC * (part + 1)] = jnp.where(same, square, 0.0).astype(BF16)

    load_s.wait()
    load_v.wait()
    for copy in load_small[1:]:
        copy.wait()

    @pl.when(buffer_slab)
    def _():
        def chunk(c, carry):
            def variable(v, inner):
                new_out[v, pl.ds(c * CR, CR), :] = fbuf[v, pl.ds(PAD + c * CR, CR), :]
                for z in range(ZN):
                    piece = fbuf[v, pl.ds(PAD + c * CR + z, YC, stride=ZN), :]
                    snap[c, z, v] = piece.astype(BF16)
                return inner

            lax.fori_loop(0, V, variable, 0)
            hand_over(c)
            return carry

        lax.fori_loop(0, NC, chunk, 0)

    @pl.when(inner_slab)
    def _():
        @pl.when(gy > 0)
        def _():
            y_copy(1).wait_recv()

        @pl.when(gy < NY - 1)
        def _():
            y_copy(0).wait_recv()

        @pl.when(ga > 0)
        def _():
            x_copy(1).wait_recv()

        x_copy(0).wait_recv()
        xcomb[...] = jnp.where(lane % 2 == 0, xrecv[0], xrecv[1])
        edge = lax.broadcasted_iota(jnp.int32, (YC, XN), 1)

        def chunk(c, carry):
            @pl.when(gz > 0)
            def _():
                z_copy(1, c).wait_recv()

            @pl.when(gz < NZ - 1)
            def _():
                z_copy(0, c).wait_recv()

            faces_sent(c)

            @pl.when(c < NC - 3)
            def _():
                start_faces(c + 3)

            for z in range(ZN):
                first = PAD + c * CR + z
                stack = jnp.concatenate(
                    [fbuf[v, pl.ds(first, YC, stride=ZN), :] for v in range(V)], axis=0
                )
                high = stack.astype(BF16)
                low = (stack - high.astype(F32)).astype(BF16)
                reacted = jnp.dot(
                    kmat[...], jnp.concatenate([high, low, high], axis=0), preferred_element_type=F32
                )
                rfb[...] = reacted.reshape(V, YC, XN)
                scale = 0.125 * time_step
                vx, vy, vz = (scale * vbuf[d, pl.ds(c * CR + z, YC, stride=ZN), :] for d in range(3))
                faces = xcomb[pl.ds(c * YC, YC), :]

                def variable(v, inner):
                    here = fbuf[v, pl.ds(first, YC, stride=ZN), :]
                    y_plus = fbuf[v, pl.ds(first + ZN, YC, stride=ZN), :]
                    y_minus = fbuf[v, pl.ds(first - ZN, YC, stride=ZN), :]
                    if z < ZN - 1:
                        z_plus = fbuf[v, pl.ds(first + 1, YC, stride=ZN), :]
                    else:
                        z_plus = zrecv[1, c, v].astype(F32)
                    if z > 0:
                        z_minus = fbuf[v, pl.ds(first - 1, YC, stride=ZN), :]
                    else:
                        z_minus = zrecv[0, c, v].astype(F32)
                    at = 2 * (v * ZN + z)
                    moved = pltpu.roll(faces, XN - 1 - at, 1)
                    x_plus = pltpu.roll(jnp.where(edge == 0, moved, here), XN - 1, 1)
                    x_minus = pltpu.roll(jnp.where(edge == XN - 1, moved, here), 1, 1)
                    laplace = (
                        (x_plus + x_minus) + (y_plus + y_minus) + (z_plus + z_minus) - 6.0 * here
                    )
                    advection = (
                        vx * (x_plus - x_minus) + vy * (y_plus - y_minus) + vz * (z_plus - z_minus)
                    )
                    began = sbuf[v, pl.ds(c * CR + z, YC, stride=ZN), :]
                    value = (
                        0.75 * began + 0.25 * here
                        + ((0.25 * time_step) * dif[v]) * laplace - advection + rfb[v]
                    )
                    new_out[v, pl.ds(c * CR + z, YC, stride=ZN), :] = value
                    snap[c, z, v] = value.astype(BF16)
                    return inner

                lax.fori_loop(0, V, variable, 0, unroll=True)
            hand_over(c)
            return carry

        lax.fori_loop(0, NC, chunk, 0)

    def project_copy(block, layer):
        slot = gy * NC + jnp.minimum(block, last)
        return bring(pbuf.at[block], mbuf.at[:, slot], ps_sem.at[block], pr_sem.at[slot], (layer, gz, layer))

    zero = jnp.zeros_like(xft[...])
    first_half = jnp.concatenate([xft[...], zero], axis=0)
    second_half = jnp.concatenate([zero, xft[...]], axis=0)
    nt = (((1,), (1,)), ((), ()))
    tn = (((0,), (0,)), ((), ()))

    def project(block):
        wide = jnp.concatenate([full[block, s].reshape(V * YC, XN) for s in range(NA)], axis=1)
        rows = V * YC // 2
        projected = lax.dot_general(wide[:rows], first_half, nt, preferred_element_type=F32)
        projected += lax.dot_general(wide[rows:], second_half, nt, preferred_element_type=F32)
        return wide, projected.astype(BF16).reshape(V // 2, YC, XN)

    def add_gram(block, wide, begin):
        for i in range(2):
            half = (core + 1 + i) % 2
            part = jnp.concatenate(
                [full[block, 2 * half + s].reshape(V * YC, XN) for s in range(2)], axis=1
            )
            term = lax.dot_general(wide, part, tn, preferred_element_type=F32)

            @pl.when(begin)
            def _():
                gacc[i] = term

            @pl.when(jnp.logical_not(begin))
            def _():
                gacc[i] = gacc[i] + term

    def own_layer(block, projected):
        @pl.when(diagonal)
        def _():
            mbuf[:, gy * NC + block] = projected

        @pl.when(jnp.logical_not(diagonal))
        def _():
            pbuf[block] = projected
            project_copy(block, ga).start()

    def gather_gram(c, carry):
        for j in range(1, NA):
            arrived(c, j).wait_recv()
        wide, projected = project(c)
        own_layer(c, projected)
        add_gram(c, wide, c == 0)
        return carry

    lax.fori_loop(0, last, gather_gram, 0)

    @pl.when(plain)
    def _():
        gather_gram(jnp.int32(last), 0)

    @pl.when(first_chip)
    def _():
        def extra(block, carry):
            for j in range(1, NA):
                last_arrived(block, j).wait_recv()
            wide, projected = project(block)

            @pl.when(block == last)
            def _():
                own_layer(block, projected)

            @pl.when(block == NC)
            def _():
                pbuf[block] = projected
                project_copy(block, ga + 2).start()

            add_gram(block, wide, block < 0)
            return carry

        lax.fori_loop(last, NC + 1, extra, 0)

    pair = bring(gacc.at[0], r1, s1_sem, r1_sem, (gy, gz, zhi * 2 + 1 - core))
    pair.start()
    pair.wait_recv()
    g2[...] = (gacc[1] + r1[...]).astype(BF16).reshape(16, 32, 256)

    def plane_copy(j):
        to = (plane + j) % 16
        return bring(g2.at[to], r2.at[plane], s2_sem.at[j], r2_sem.at[plane], plane_device(to))

    def plane_arrived(j):
        source = (plane + j) % 16
        return bring(g2.at[source], r2.at[source], s2_sem.at[j], r2_sem.at[source], plane_device(source))

    def start_plane(j, carry):
        plane_copy(j).start()
        return carry

    for j in range(1, 16):
        start_plane(j, 0)

    def bcast_copy(j):
        peer = (ga + j) % NA
        return bring(ysend, yrecv, bs_sem.at[j], br_sem, (gy, gz, peer))

    @pl.when(diagonal)
    def _():
        def wait_projected(i, carry):
            slot = (gy * NC + i) % 16
            bring(
                pbuf.at[0], mbuf.at[:, slot], ps_sem.at[0], pr_sem.at[slot], ((ga + 1) % NA, gz, ga)
            ).wait_recv()
            return carry

        @pl.when(second_chip)
        def _():
            wait_projected(last, 0)

        lax.fori_loop(NC, 16, wait_projected, 0)
        y_gram = jnp.zeros((256, 256), F32)
        for i in range(V // 2):
            layer = mbuf[i].reshape(256, XN)
            y_gram += lax.dot_general(layer, layer, nt, preferred_element_type=F32)
        product = jnp.dot(
            yft[...], y_gram * (1.0 / 1024.0), precision=lax.Precision.HIGHEST, preferred_element_type=F32
        )
        ysend[...] = product
        yprod_out[...] = product
        for j in (2, 3, 1):
            bcast_copy(j).start()

    def add_plane(j, acc):
        plane_arrived(j).wait_recv()
        return acc + r2[(plane + j) % 16].astype(F32)

    total = g2[plane].astype(F32)
    for j in range(1, 16):
        total = add_plane(j, total)
    s2[...] = total.reshape(4, 8, 256)
    r3[column] = s2[cz]

    def column_copy(j):
        to = (column + j) % 16
        return bring(s2.at[(to // 2) % 4], r3.at[column], s3_sem.at[j], r3_sem.at[column], column_device(to))

    def column_arrived(j):
        source = (column + j) % 16
        return bring(s2.at[0], r3.at[source], s3_sem.at[j], r3_sem.at[source], column_device(source))

    def start_column(j, carry):
        column_copy(j).start()
        return carry

    for j in range(1, 16):
        start_column(j, 0)

    @pl.when(low_y)
    def _():
        y_copy(0).wait_send()

    @pl.when(high_y)
    def _():
        y_copy(1).wait_send()

    @pl.when(low_x)
    def _():
        x_copy(0).wait_send()

    @pl.when(high_x)
    def _():
        x_copy(1).wait_send()

    def sent(c, carry):
        for j in range(1, NA):
            exchange(c, j).wait_send()

        @pl.when(jnp.logical_not(diagonal))
        def _():
            project_copy(c, ga).wait_send()

        return carry

    lax.fori_loop(0, last, sent, 0)

    @pl.when(plain)
    def _():
        sent(last, 0)

    @pl.when(first_chip)
    def _():
        for m in range(2):
            last_swap(m).wait_send()

        @pl.when(jnp.logical_not(diagonal))
        def _():
            project_copy(last, ga).wait_send()

        project_copy(NC, ga + 2).wait_send()

    @pl.when(second_chip)
    def _():
        for layer in range(NA):
            last_exchange(layer).wait_send()

    pair.wait_send()

    def plane_sent(j, carry):
        plane_copy(j).wait_send()
        return carry

    for j in range(1, 16):
        plane_sent(j, 0)

    @pl.when(diagonal)
    def _():
        for j in range(1, NA):
            bcast_copy(j).wait_send()

    @pl.when(jnp.logical_not(diagonal))
    def _():
        bcast_copy(1).wait_recv()
        yprod_out[...] = yrecv[...]

    def column_wait(j, carry):
        column_arrived(j).wait_recv()
        return carry

    for j in range(1, 16):
        column_wait(j, 0)
    cells = 1.0 / float(V * 256 * 64)
    for half in range(2):
        acc = r3[half]
        for z in range(1, 8):
            acc = acc + r3[2 * z + half]
        gram_out[:, 256 * half : 256 * (half + 1)] = acc * cells

    def column_sent(j, carry):
        column_copy(j).wait_send()
        return carry

    for j in range(1, 16):
        column_sent(j, 0)


def finish(new, gram, product, new_out, gram_out, product_out, sem):
    copies = [
        pltpu.make_async_copy(src, dst, sem.at[i])
        for i, (src, dst) in enumerate(((new, new_out), (gram, gram_out), (product, product_out)))
    ]
    for copy in copies:
        copy.start()
    for copy in copies:
        copy.wait()


def shards(fields, section_start, velocity, diffusivity, reaction, x_factor, y_factor):
    vmem = pl.BlockSpec(memory_space=pltpu.VMEM)
    hbm = pl.BlockSpec(memory_space=pltpu.HBM)
    dma = pltpu.SemaphoreType.DMA
    new_fields, gram, product = pl.pallas_call(
        kernel,
        out_shape=(
            pltpu.VMEM((V, ROWS, XN), F32),
            pltpu.VMEM((8, 512), F32),
            pltpu.VMEM((64, 256), F32),
        ),
        in_specs=[hbm] * 7,
        out_specs=(vmem, vmem, vmem),
        scratch_shapes=[
            pltpu.SMEM((V,), F32),
            pltpu.VMEM((V, V), F32),
            pltpu.VMEM((64, 512), BF16),
            pltpu.VMEM((64, 256), F32),
            pltpu.VMEM((V, PAD + ROWS + PAD, XN), F32),
            pltpu.VMEM((V, ROWS, XN), F32),
            pltpu.VMEM((3, ROWS, XN), F32),
            pltpu.VMEM((2, NC, V, YC, XN), BF16),
            pltpu.VMEM((2, NC, V, YC, XN), BF16),
            pltpu.VMEM((YN, XN), F32),
            pltpu.VMEM((2, YN, XN), F32),
            pltpu.VMEM((YN, XN), F32),
            pltpu.VMEM((NC, ZN, V, YC, XN), BF16),
            pltpu.VMEM((NC + 1, NA, V, YC, XN), BF16),
            pltpu.VMEM((V * YC, 3 * V * YC), BF16),
            pltpu.VMEM((V, YC, XN), F32),
            pltpu.VMEM((2, 512, 256), F32),
            pltpu.VMEM((512, 256), F32),
            pltpu.VMEM((16, 32, 256), BF16),
            pltpu.VMEM((16, 32, 256), BF16),
            pltpu.VMEM((4, 8, 256), F32),
            pltpu.VMEM((16, 8, 256), F32),
            pltpu.VMEM((NC + 1, V // 2, YC, XN), BF16),
            pltpu.VMEM((V // 2, 16, YC, XN), BF16),
            pltpu.VMEM((64, 256), F32),
            pltpu.VMEM((64, 256), F32),
            dma((7,)),
            dma((2, NC)), dma((2, NC)), dma((2,)), dma((2,)), dma((2,)), dma((2,)),
            dma((NC, NA)), dma((NC + 1, NA)),
            dma((NC + 1,)), dma((16,)), dma((NA,)), dma,
            dma, dma, dma((16,)), dma((16,)), dma((16,)), dma((16,)),
        ],
        compiler_params=pltpu.CompilerParams(
            collective_id=0, has_side_effects=True, vmem_limit_bytes=24 << 20
        ),
        name="section",
    )(
        *(
            pltpu.with_memory_space_constraint(array, pltpu.HBM)
            for array in (
                diffusivity,
                reaction,
                x_factor.T,
                y_factor.T,
                fields.reshape(V, ROWS, XN),
                section_start.reshape(V, ROWS, XN),
                velocity.reshape(3, ROWS, XN),
            )
        )
    )
    new_fields, gram, product = pl.pallas_call(
        finish,
        out_shape=(
            jax.ShapeDtypeStruct((V, ROWS, XN), F32),
            jax.ShapeDtypeStruct((8, 512), F32),
            jax.ShapeDtypeStruct((64, 256), F32),
        ),
        in_specs=[pl.BlockSpec(memory_space=pl.ANY)] * 3,
        out_specs=(hbm,) * 3,
        scratch_shapes=[dma((3,))],
        name="finish", compiler_params=pltpu.CompilerParams(vmem_limit_bytes=1 << 20),
    )(new_fields, gram, product)
    return new_fields.reshape(V, YN, ZN, XN), gram, product.T[None]


def solution(mesh):
    in_specs = (
        P(None, "gy", "gz", "ga"),
        P(None, "gy", "gz", "ga"),
        P(None, "gy", "gz", "ga"),
        P(),
        P(),
        P(),
        P(),
    )
    out_specs = (P(None, "gy", "gz", "ga"), P(("gy", "gz"), None), P(("gz", "gy"), None, None))
    return jax.shard_map(shards, mesh=mesh, in_specs=in_specs, out_specs=out_specs, check_vma=False)
```

```python
import functools

import jax
import jax.numpy as jnp
from jax import lax
from jax.experimental import pallas as pl
from jax.experimental.pallas import tpu as pltpu
from jax.sharding import PartitionSpec as P

time_step = 0.4

MESH = pl.DeviceIdType.MESH
V = 16
YN = 64
ZN = 4
XN = 128
ROWS = YN * ZN
NC = 4
YC = YN // NC
CR = YC * ZN
PAD = 8
NY, NZ, NA = 4, 16, 4
F32, BF16 = jnp.float32, jnp.bfloat16


def bring(src, dst, send_sem, recv_sem, device):
    return pltpu.make_async_remote_copy(
        src_ref=src, dst_ref=dst, send_sem=send_sem, recv_sem=recv_sem, device_id=device, device_id_type=MESH
    )


def kernel(
    dif_in, rea_in, xft_in, yft_in, fields, start, vel,
    new_out, gram_out, yprod_out,
    dif, rea, xft, yft, fbuf, sbuf, vbuf, zsend, zrecv, xpack, xrecv, xcomb, snap, full, kmat, rfb,
    gacc, r1, g2, r2, s2, r3, pbuf, mbuf, ysend, yrecv,
    load_sem, zs_sem, zr_sem, ys_sem, yr_sem, xs_sem, xr_sem, as_sem, ar_sem,
    ps_sem, pr_sem, bs_sem, br_sem, s1_sem, r1_sem, s2_sem, r2_sem, s3_sem, r3_sem,
):
    gy, gz, ga = lax.axis_index("gy"), lax.axis_index("gz"), lax.axis_index("ga")
    cy, cz = gz // 4, gz % 4
    zhi, core = ga // 2, ga % 2
    plane = gy * 4 + cy
    column = (zhi * 4 + cz) * 2 + core
    buffer_slab = ga == NA - 1
    diagonal = gy == ga
    at_end = jnp.logical_or(cz == 0, cz == 3)
    plain = jnp.logical_not(at_end)
    first_chip = jnp.logical_and(at_end, zhi == 0)
    second_chip = jnp.logical_and(at_end, zhi == 1)
    to_second = jnp.logical_and(first_chip, gy != ga + 2)
    from_first = jnp.logical_and(second_chip, diagonal)
    inner_slab = ga < NA - 1

    def plane_device(index):
        return (index // 4, (index % 4) * 4 + cz, ga)

    def column_device(index):
        return (gy, cy * 4 + (index // 2) % 4, (index // 8) * 2 + index % 2)

    barrier = pltpu.get_barrier_semaphore()
    wrap_up = jnp.logical_and(cz == 3, gz < NZ - 1)
    wrap_down = jnp.logical_and(cz == 0, gz > 0)

    @pl.when(wrap_up)
    def _():
        pl.semaphore_signal(barrier, inc=1, device_id=(gy, gz + 1, ga), device_id_type=MESH)

    @pl.when(wrap_down)
    def _():
        pl.semaphore_signal(barrier, inc=1, device_id=(gy, gz - 1, ga), device_id_type=MESH)

    def greet(j, carry):
        pl.semaphore_signal(barrier, inc=1, device_id=plane_device((plane + j) % 16), device_id_type=MESH)
        pl.semaphore_signal(barrier, inc=1, device_id=column_device((column + j) % 16), device_id_type=MESH)
        return carry

    for j in (8, 9, 7, 10, 6, 11, 5, 12, 4, 13, 3, 14, 2, 15, 1):
        greet(j, 0)

    @pl.when(to_second)
    def _():
        pl.semaphore_signal(barrier, inc=1, device_id=(ga + 2, gz, ga + 2), device_id_type=MESH)

    @pl.when(from_first)
    def _():
        for j in range(1, NY):
            pl.semaphore_signal(barrier, inc=1, device_id=((gy + j) % NY, gz, ga - 2), device_id_type=MESH)

    load_f = pltpu.make_async_copy(fields, fbuf.at[:, pl.ds(PAD, ROWS), :], load_sem.at[0])
    load_s = pltpu.make_async_copy(start, sbuf, load_sem.at[1])
    load_v = pltpu.make_async_copy(vel, vbuf, load_sem.at[2])
    load_small = [
        pltpu.make_async_copy(src, dst, load_sem.at[3 + i])
        for i, (src, dst) in enumerate(((rea_in, rea), (dif_in, dif), (xft_in, xft), (yft_in, yft)))
    ]
    load_f.start()
    load_small[0].start()
    load_s.start()
    load_v.start()
    for copy in load_small[1:]:
        copy.start()

    @pl.when(gy == 0)
    def _():
        fbuf[:, 0:PAD, :] = jnp.zeros((V, PAD, XN), F32)

    @pl.when(gy == NY - 1)
    def _():
        fbuf[:, PAD + ROWS : PAD + ROWS + PAD, :] = jnp.zeros((V, PAD, XN), F32)

    @pl.when(gz == 0)
    def _():
        zrecv[0] = jnp.zeros((NC, V, YC, XN), BF16)

    @pl.when(gz == NZ - 1)
    def _():
        zrecv[1] = jnp.zeros((NC, V, YC, XN), BF16)

    @pl.when(ga == 0)
    def _():
        xrecv[0] = jnp.zeros((YN, XN), F32)

    load_f.wait()

    @pl.when(inner_slab)
    def _():
        def face(v, carry):
            for side, z in ((0, 0), (1, ZN - 1)):
                for c in range(NC):
                    piece = fbuf[v, pl.ds(PAD + c * CR + z, YC, stride=ZN), :]
                    zsend[side, c, v] = piece.astype(BF16)
            return carry

        lax.fori_loop(0, V, face, 0)

    pl.semaphore_wait(
        barrier,
        30 + wrap_up.astype(jnp.int32) + wrap_down.astype(jnp.int32)
        + to_second.astype(jnp.int32) + 3 * from_first.astype(jnp.int32),
    )

    def z_copy(side, c):
        return bring(
            zsend.at[side, c], zrecv.at[1 - side, c], zs_sem.at[side, c], zr_sem.at[1 - side, c],
            (gy, gz - 1 + 2 * side, ga),
        )

    low_z = jnp.logical_and(inner_slab, gz > 0)
    high_z = jnp.logical_and(inner_slab, gz < NZ - 1)
    low_y = jnp.logical_and(inner_slab, gy > 0)
    high_y = jnp.logical_and(inner_slab, gy < NY - 1)

    def y_copy(side):
        src = fields.at[:, pl.ds((ROWS - PAD) * side, PAD), :]
        dst = fbuf.at[:, pl.ds((PAD + ROWS) * (1 - side), PAD), :]
        return bring(src, dst, ys_sem.at[side], yr_sem.at[1 - side], (gy - 1 + 2 * side, gz, ga))

    def start_faces(c):
        @pl.when(low_z)
        def _():
            z_copy(0, c).start()

        @pl.when(high_z)
        def _():
            z_copy(1, c).start()

    def faces_sent(c):
        @pl.when(low_z)
        def _():
            z_copy(0, c).wait_send()

        @pl.when(high_z)
        def _():
            z_copy(1, c).wait_send()

    start_faces(0)

    @pl.when(low_y)
    def _():
        y_copy(0).start()

    @pl.when(high_y)
    def _():
        y_copy(1).start()

    lane = lax.broadcasted_iota(jnp.int32, (YN, XN), 1)

    def pack(v, acc):
        for z in range(ZN):
            at = 2 * (v * ZN + z)
            piece = fbuf[v, pl.ds(PAD + z, YN, stride=ZN), :]
            moved = pltpu.roll(piece, at + 1, 1)
            acc = jnp.where(jnp.logical_or(lane == at, lane == at + 1), moved, acc)
        return acc

    xpack[...] = lax.fori_loop(0, V, pack, jnp.zeros((YN, XN), F32))

    def x_copy(side):
        return bring(
            xpack, xrecv.at[1 - side], xs_sem.at[side], xr_sem.at[1 - side], (gy, gz, ga - 1 + 2 * side)
        )

    low_x = ga > 0
    high_x = ga < NA - 2

    @pl.when(low_x)
    def _():
        x_copy(0).start()

    @pl.when(high_x)
    def _():
        x_copy(1).start()

    start_faces(1)
    start_faces(2)

    def exchange(c, j):
        peer = (ga + j) % NA
        return bring(snap.at[c, peer], full.at[c, ga], as_sem.at[c, j], ar_sem.at[c, ga], (gy, gz, peer))

    def arrived(c, j):
        slab = (ga + j) % NA
        return bring(snap.at[c, slab], full.at[c, slab], as_sem.at[c, j], ar_sem.at[c, slab], (gy, gz, slab))

    last = NC - 1

    def last_exchange(layer):
        return bring(
            snap.at[last, layer], full.at[last + layer // 2, ga], as_sem.at[last, layer],
            ar_sem.at[last + layer // 2, ga], (gy, gz, layer % 2),
        )

    def last_swap(m):
        return bring(
            snap.at[last, 2 * m + 1 - core], full.at[last + m, ga], as_sem.at[last, m],
            ar_sem.at[last + m, ga], (gy, gz, 1 - core),
        )

    def last_arrived(block, j):
        slab = (ga + j) % NA
        return bring(
            snap.at[0, slab], full.at[block, slab], as_sem.at[0, j], ar_sem.at[block, slab], (gy, gz, slab)
        )

    def hand_over(c):
        @pl.when(jnp.logical_or(plain, c < last))
        def _():
            full[c, ga] = snap[c, ga]
            for j in (2, 3, 1):
                exchange(c, j).start()

        @pl.when(jnp.logical_and(c == last, first_chip))
        def _():
            for m in range(2):
                last_swap(m).start()
            for m in range(2):
                full[last + m, ga] = snap[last, 2 * m + core]

        @pl.when(jnp.logical_and(c == last, second_chip))
        def _():
            for layer in range(NA):
                last_exchange(layer).start()

    load_small[0].wait()

    low16 = lax.broadcasted_iota(jnp.int32, (V * YC, V), 0) // YC
    spread = (low16 == lax.broadcasted_iota(jnp.int32, (V * YC, V), 1)).astype(F32).astype(BF16)
    rows_at = lax.broadcasted_iota(jnp.int32, (V * YC, V * YC), 0) % YC
    cols_at = lax.broadcasted_iota(jnp.int32, (V * YC, V * YC), 1) % YC
    same = rows_at == cols_at
    rate = (0.25 * time_step) * rea[...]
    rate_high = rate.astype(BF16)
    rate_low = (rate - rate_high.astype(F32)).astype(BF16)
    for part, piece in enumerate((rate_high, rate_high, rate_low)):
        tall = jnp.dot(spread, piece, preferred_element_type=F32).astype(BF16)
        square = lax.dot_general(tall, spread, (((1,), (1,)), ((), ())), preferred_element_type=F32)
        kmat[:, V * YC * part : V * YC * (part + 1)] = jnp.where(same, square, 0.0).astype(BF16)

    load_s.wait()
    load_v.wait()
    for copy in load_small[1:]:
        copy.wait()

    @pl.when(buffer_slab)
    def _():
        def chunk(c, carry):
            def variable(v, inner):
                new_out[v, pl.ds(c * CR, CR), :] = fbuf[v, pl.ds(PAD + c * CR, CR), :]
                for z in range(ZN):
                    piece = fbuf[v, pl.ds(PAD + c * CR + z, YC, stride=ZN), :]
                    snap[c, z, v] = piece.astype(BF16)
                return inner

            lax.fori_loop(0, V, variable, 0)
            hand_over(c)
            return carry

        lax.fori_loop(0, NC, chunk, 0)

    @pl.when(inner_slab)
    def _():
        @pl.when(gy > 0)
        def _():
            y_copy(1).wait_recv()

        @pl.when(gy < NY - 1)
        def _():
            y_copy(0).wait_recv()

        @pl.when(ga > 0)
        def _():
            x_copy(1).wait_recv()

        x_copy(0).wait_recv()
        xcomb[...] = jnp.where(lane % 2 == 0, xrecv[0], xrecv[1])
        edge = lax.broadcasted_iota(jnp.int32, (YC, XN), 1)

        def chunk(c, carry):
            @pl.when(gz > 0)
            def _():
                z_copy(1, c).wait_recv()

            @pl.when(gz < NZ - 1)
            def _():
                z_copy(0, c).wait_recv()

            faces_sent(c)

            @pl.when(c < NC - 3)
            def _():
                start_faces(c + 3)

            for z in range(ZN):
                first = PAD + c * CR + z
                stack = jnp.concatenate(
                    [fbuf[v, pl.ds(first, YC, stride=ZN), :] for v in range(V)], axis=0
                )
                high = stack.astype(BF16)
                low = (stack - high.astype(F32)).astype(BF16)
                reacted = jnp.dot(
                    kmat[...], jnp.concatenate([high, low, high], axis=0), preferred_element_type=F32
                )
                rfb[...] = reacted.reshape(V, YC, XN)
                scale = 0.125 * time_step
                vx, vy, vz = (scale * vbuf[d, pl.ds(c * CR + z, YC, stride=ZN), :] for d in range(3))
                faces = xcomb[pl.ds(c * YC, YC), :]

                def variable(v, inner):
                    here = fbuf[v, pl.ds(first, YC, stride=ZN), :]
                    y_plus = fbuf[v, pl.ds(first + ZN, YC, stride=ZN), :]
                    y_minus = fbuf[v, pl.ds(first - ZN, YC, stride=ZN), :]
                    if z < ZN - 1:
                        z_plus = fbuf[v, pl.ds(first + 1, YC, stride=ZN), :]
                    else:
                        z_plus = zrecv[1, c, v].astype(F32)
                    if z > 0:
                        z_minus = fbuf[v, pl.ds(first - 1, YC, stride=ZN), :]
                    else:
                        z_minus = zrecv[0, c, v].astype(F32)
                    at = 2 * (v * ZN + z)
                    moved = pltpu.roll(faces, XN - 1 - at, 1)
                    x_plus = pltpu.roll(jnp.where(edge == 0, moved, here), XN - 1, 1)
                    x_minus = pltpu.roll(jnp.where(edge == XN - 1, moved, here), 1, 1)
                    laplace = (
                        (x_plus + x_minus) + (y_plus + y_minus) + (z_plus + z_minus) - 6.0 * here
                    )
                    advection = (
                        vx * (x_plus - x_minus) + vy * (y_plus - y_minus) + vz * (z_plus - z_minus)
                    )
                    began = sbuf[v, pl.ds(c * CR + z, YC, stride=ZN), :]
                    value = (
                        0.75 * began + 0.25 * here
                        + ((0.25 * time_step) * dif[v]) * laplace - advection + rfb[v]
                    )
                    new_out[v, pl.ds(c * CR + z, YC, stride=ZN), :] = value
                    snap[c, z, v] = value.astype(BF16)
                    return inner

                lax.fori_loop(0, V, variable, 0, unroll=True)
            hand_over(c)
            return carry

        lax.fori_loop(0, NC, chunk, 0)

    def project_copy(block, layer):
        slot = gy * NC + jnp.minimum(block, last)
        return bring(pbuf.at[block], mbuf.at[:, slot], ps_sem.at[block], pr_sem.at[slot], (layer, gz, layer))

    zero = jnp.zeros_like(xft[...])
    first_half = jnp.concatenate([xft[...], zero], axis=0)
    second_half = jnp.concatenate([zero, xft[...]], axis=0)
    nt = (((1,), (1,)), ((), ()))
    tn = (((0,), (0,)), ((), ()))

    def project(block):
        wide = jnp.concatenate([full[block, s].reshape(V * YC, XN) for s in range(NA)], axis=1)
        rows = V * YC // 2
        projected = lax.dot_general(wide[:rows], first_half, nt, preferred_element_type=F32)
        projected += lax.dot_general(wide[rows:], second_half, nt, preferred_element_type=F32)
        return wide, projected.astype(BF16).reshape(V // 2, YC, XN)

    def add_gram(block, wide, begin):
        for i in range(2):
            half = (core + 1 + i) % 2
            part = jnp.concatenate(
                [full[block, 2 * half + s].reshape(V * YC, XN) for s in range(2)], axis=1
            )
            term = lax.dot_general(wide, part, tn, preferred_element_type=F32)

            @pl.when(begin)
            def _():
                gacc[i] = term

            @pl.when(jnp.logical_not(begin))
            def _():
                gacc[i] = gacc[i] + term

    def own_layer(block, projected):
        @pl.when(diagonal)
        def _():
            mbuf[:, gy * NC + block] = projected

        @pl.when(jnp.logical_not(diagonal))
        def _():
            pbuf[block] = projected
            project_copy(block, ga).start()

    def gather_gram(c, carry):
        for j in range(1, NA):
            arrived(c, j).wait_recv()
        wide, projected = project(c)
        own_layer(c, projected)
        add_gram(c, wide, c == 0)
        return carry

    lax.fori_loop(0, last, gather_gram, 0)

    @pl.when(plain)
    def _():
        gather_gram(jnp.int32(last), 0)

    @pl.when(first_chip)
    def _():
        def extra(block, carry):
            for j in range(1, NA):
                last_arrived(block, j).wait_recv()
            wide, projected = project(block)

            @pl.when(block == last)
            def _():
                own_layer(block, projected)

            @pl.when(block == NC)
            def _():
                pbuf[block] = projected
                project_copy(block, ga + 2).start()

            add_gram(block, wide, block < 0)
            return carry

        lax.fori_loop(last, NC + 1, extra, 0)

    pair = bring(gacc.at[0], r1, s1_sem, r1_sem, (gy, gz, zhi * 2 + 1 - core))
    pair.start()
    pair.wait_recv()
    g2[...] = (gacc[1] + r1[...]).astype(BF16).reshape(16, 32, 256)

    def plane_copy(j):
        to = (plane + j) % 16
        return bring(g2.at[to], r2.at[plane], s2_sem.at[j], r2_sem.at[plane], plane_device(to))

    def plane_arrived(j):
        source = (plane + j) % 16
        return bring(g2.at[source], r2.at[source], s2_sem.at[j], r2_sem.at[source], plane_device(source))

    def start_plane(j, carry):
        plane_copy(j).start()
        return carry

    for j in range(1, 16):
        start_plane(j, 0)

    def bcast_copy(j):
        peer = (ga + j) % NA
        return bring(ysend, yrecv, bs_sem.at[j], br_sem, (gy, gz, peer))

    @pl.when(diagonal)
    def _():
        def wait_projected(i, carry):
            slot = (gy * NC + i) % 16
            bring(
                pbuf.at[0], mbuf.at[:, slot], ps_sem.at[0], pr_sem.at[slot], ((ga + 1) % NA, gz, ga)
            ).wait_recv()
            return carry

        @pl.when(second_chip)
        def _():
            wait_projected(last, 0)

        lax.fori_loop(NC, 16, wait_projected, 0)
        y_gram = jnp.zeros((256, 256), F32)
        for i in range(V // 2):
            layer = mbuf[i].reshape(256, XN)
            y_gram += lax.dot_general(layer, layer, nt, preferred_element_type=F32)
        product = jnp.dot(
            yft[...], y_gram * (1.0 / 1024.0), precision=lax.Precision.HIGHEST, preferred_element_type=F32
        )
        ysend[...] = product
        yprod_out[...] = product
        for j in (2, 3, 1):
            bcast_copy(j).start()

    def add_plane(j, acc):
        plane_arrived(j).wait_recv()
        return acc + r2[(plane + j) % 16].astype(F32)

    total = g2[plane].astype(F32)
    for j in range(1, 16):
        total = add_plane(j, total)
    s2[...] = total.reshape(4, 8, 256)
    r3[column] = s2[cz]

    def column_copy(j):
        to = (column + j) % 16
        return bring(s2.at[(to // 2) % 4], r3.at[column], s3_sem.at[j], r3_sem.at[column], column_device(to))

    def column_arrived(j):
        source = (column + j) % 16
        return bring(s2.at[0], r3.at[source], s3_sem.at[j], r3_sem.at[source], column_device(source))

    def start_column(j, carry):
        column_copy(j).start()
        return carry

    for j in range(1, 16):
        start_column(j, 0)

    @pl.when(low_y)
    def _():
        y_copy(0).wait_send()

    @pl.when(high_y)
    def _():
        y_copy(1).wait_send()

    @pl.when(low_x)
    def _():
        x_copy(0).wait_send()

    @pl.when(high_x)
    def _():
        x_copy(1).wait_send()

    def sent(c, carry):
        for j in range(1, NA):
            exchange(c, j).wait_send()

        @pl.when(jnp.logical_not(diagonal))
        def _():
            project_copy(c, ga).wait_send()

        return carry

    lax.fori_loop(0, last, sent, 0)

    @pl.when(plain)
    def _():
        sent(last, 0)

    @pl.when(first_chip)
    def _():
        for m in range(2):
            last_swap(m).wait_send()

        @pl.when(jnp.logical_not(diagonal))
        def _():
            project_copy(last, ga).wait_send()

        project_copy(NC, ga + 2).wait_send()

    @pl.when(second_chip)
    def _():
        for layer in range(NA):
            last_exchange(layer).wait_send()

    pair.wait_send()

    def plane_sent(j, carry):
        plane_copy(j).wait_send()
        return carry

    for j in range(1, 16):
        plane_sent(j, 0)

    @pl.when(diagonal)
    def _():
        for j in range(1, NA):
            bcast_copy(j).wait_send()

    @pl.when(jnp.logical_not(diagonal))
    def _():
        bcast_copy(1).wait_recv()
        yprod_out[...] = yrecv[...]

    def column_wait(j, carry):
        column_arrived(j).wait_recv()
        return carry

    for j in range(1, 16):
        column_wait(j, 0)
    cells = 1.0 / float(V * 256 * 64)
    for half in range(2):
        acc = r3[half]
        for z in range(1, 8):
            acc = acc + r3[2 * z + half]
        gram_out[:, 256 * half : 256 * (half + 1)] = acc * cells

    def column_sent(j, carry):
        column_copy(j).wait_send()
        return carry

    for j in range(1, 16):
        column_sent(j, 0)


def finish(new, gram, product, new_out, gram_out, product_out, sem):
    copies = [
        pltpu.make_async_copy(src, dst, sem.at[i])
        for i, (src, dst) in enumerate(((new, new_out), (gram, gram_out), (product, product_out)))
    ]
    for copy in copies:
        copy.start()
    for copy in copies:
        copy.wait()


def shards(fields, section_start, velocity, diffusivity, reaction, x_factor, y_factor):
    vmem = pl.BlockSpec(memory_space=pltpu.VMEM)
    hbm = pl.BlockSpec(memory_space=pltpu.HBM)
    dma = pltpu.SemaphoreType.DMA
    new_fields, gram, product = pl.pallas_call(
        kernel,
        out_shape=(
            pltpu.VMEM((V, ROWS, XN), F32),
            pltpu.VMEM((8, 512), F32),
            pltpu.VMEM((64, 256), F32),
        ),
        in_specs=[hbm] * 7,
        out_specs=(vmem, vmem, vmem),
        scratch_shapes=[
            pltpu.SMEM((V,), F32),
            pltpu.VMEM((V, V), F32),
            pltpu.VMEM((64, 512), BF16),
            pltpu.VMEM((64, 256), F32),
            pltpu.VMEM((V, PAD + ROWS + PAD, XN), F32),
            pltpu.VMEM((V, ROWS, XN), F32),
            pltpu.VMEM((3, ROWS, XN), F32),
            pltpu.VMEM((2, NC, V, YC, XN), BF16),
            pltpu.VMEM((2, NC, V, YC, XN), BF16),
            pltpu.VMEM((YN, XN), F32),
            pltpu.VMEM((2, YN, XN), F32),
            pltpu.VMEM((YN, XN), F32),
            pltpu.VMEM((NC, ZN, V, YC, XN), BF16),
            pltpu.VMEM((NC + 1, NA, V, YC, XN), BF16),
            pltpu.VMEM((V * YC, 3 * V * YC), BF16),
            pltpu.VMEM((V, YC, XN), F32),
            pltpu.VMEM((2, 512, 256), F32),
            pltpu.VMEM((512, 256), F32),
            pltpu.VMEM((16, 32, 256), BF16),
            pltpu.VMEM((16, 32, 256), BF16),
            pltpu.VMEM((4, 8, 256), F32),
            pltpu.VMEM((16, 8, 256), F32),
            pltpu.VMEM((NC + 1, V // 2, YC, XN), BF16),
            pltpu.VMEM((V // 2, 16, YC, XN), BF16),
            pltpu.VMEM((64, 256), F32),
            pltpu.VMEM((64, 256), F32),
            dma((7,)),
            dma((2, NC)), dma((2, NC)), dma((2,)), dma((2,)), dma((2,)), dma((2,)),
            dma((NC, NA)), dma((NC + 1, NA)),
            dma((NC + 1,)), dma((16,)), dma((NA,)), dma,
            dma, dma, dma((16,)), dma((16,)), dma((16,)), dma((16,)),
        ],
        compiler_params=pltpu.CompilerParams(
            collective_id=0, has_side_effects=True, vmem_limit_bytes=24 << 20
        ),
        name="section",
    )(
        *(
            pltpu.with_memory_space_constraint(array, pltpu.HBM)
            for array in (
                diffusivity,
                reaction,
                x_factor.T,
                y_factor.T,
                fields.reshape(V, ROWS, XN),
                section_start.reshape(V, ROWS, XN),
                velocity.reshape(3, ROWS, XN),
            )
        )
    )
    new_fields, gram, product = pl.pallas_call(
        finish,
        out_shape=(
            jax.ShapeDtypeStruct((V, ROWS, XN), F32),
            jax.ShapeDtypeStruct((8, 512), F32),
            jax.ShapeDtypeStruct((64, 256), F32),
        ),
        in_specs=[pl.BlockSpec(memory_space=pl.ANY)] * 3,
        out_specs=(hbm,) * 3,
        scratch_shapes=[dma((3,))],
        name="finish", compiler_params=pltpu.CompilerParams(vmem_limit_bytes=1 << 20),
    )(new_fields, gram, product)
    return new_fields.reshape(V, YN, ZN, XN), gram, product.T[None]


def solution(mesh):
    in_specs = (
        P(None, "gy", "gz", "ga"),
        P(None, "gy", "gz", "ga"),
        P(None, "gy", "gz", "ga"),
        P(),
        P(),
        P(),
        P(),
    )
    out_specs = (P(None, "gy", "gz", "ga"), P(("gy", "gz"), None), P(("gz", "gy"), None, None))
    return jax.shard_map(shards, mesh=mesh, in_specs=in_specs, out_specs=out_specs, check_vma=False)
```
